32 devices in a mesh: groups: 2 (over y), tiles: 4 (over z), depth: 2 (over x), sub: 2 (over core).
Axes of the slice: x: 2, y: 2, z: 4, core: 2. Of those that a mesh axis runs over, the one named last changes fastest.
Arguments:
- state_init: float32 [8, 4, 16, 4096], P('groups', 'depth', 'tiles', 'sub'), parts along dimension 0, may hold values from -6 to 6
- cotangent: float32 [8, 4, 16, 4096], P('groups', 'depth', 'tiles', 'sub'), parts along dimension 0, may hold values from -6 to 6
- level_count: int32 [16, 4096], P('tiles', 'sub'), may hold values from 0 to 4, as said below
- west_east: int32 [16, 2], P('tiles'), may hold values from -1 to 15, as said below
- south_north: int32 [16, 2], P('tiles'), may hold values from -1 to 3, as said below
- weight_in: bfloat16 [128, 12], replicated, may hold values from -1.75 to 1.75
- bias_in: float32 [128], replicated, may hold values from -3 to 3
- weight_mid: bfloat16 [128, 128], replicated, may hold values from -0.5 to 0.5
- bias_mid: float32 [128], replicated, may hold values from -3 to 3
- weight_out: bfloat16 [4, 128], replicated, may hold values from -0.5 to 0.5
- bias_out: float32 [4], replicated, may hold values from -3 to 3
- mix_horizontal: float32 [4], replicated, may hold values from 0.03 to 0.12
- mix_vertical: float32 [4], P('depth'), may hold values from 0.05 to 0.25
Outputs:
- final_state: float32 [8, 4, 16, 4096], P('groups', 'depth', 'tiles', 'sub'), parts along dimension 0
- initial_cot: float32 [8, 4, 16, 4096], P('groups', 'depth', 'tiles', 'sub'), parts along dimension 0
- grad_weight_in: float32 [256, 12], P('groups'), parts along dimension 0
- grad_bias_in: float32 [256], P('groups'), parts along dimension 0
- grad_weight_mid: float32 [256, 128], P('groups'), parts along dimension 0
- grad_bias_mid: float32 [256], P('groups'), parts along dimension 0
- grad_weight_out: float32 [8, 128], P('groups'), parts along dimension 0
- grad_bias_out: float32 [8], P('groups'), parts along dimension 0
The draws below stay inside these ranges and needn't reach their ends.
There are 2 independent parts, one for each index of `groups`. The reference program is written for one: setup_inputs(seed, part) draws one part's arguments, and reference() takes and returns one part's arrays. A program takes and returns all parts, laid end to end along the dimension named above; an argument that names none is the same for every part. Nothing has to cross between parts.
Inputs may be any that keep to these rules, and one draw needn't show every extreme that they name: Level k of column c of slot g is ocean where k < level_count[g, c]; 0 is land. A slot that holds no ocean tile is 0 in every column. `west_east`: entry [g, 0] is the slot of the tile that borders slot g on the west and [g, 1] the one on the east, or -1 where there is none, where the edge between them is closed, or where either of the two holds no ocean tile. The relation is mutual: b is the west neighbour of g exactly when g is the east neighbour of b, and a tile never borders itself. Call slots t * 4 to t * 4 + 3 a group; of the tiles of one group, at most 2 are west or east neighbours of tiles of one other group, and some pair of groups reaches 2 in every draw. `south_north`: entry [g, 0] gives the tile on the south of slot g and [g, 1] the one on the north, as a position among the slots of the same group (the tile in slot g - g % 4 + entry), or -1 where there is none, where the edge between them is closed, or where either of the two holds no ocean tile. The relation is mutual.
All inputs are finite; a program needn't handle non-finite values.
Results may differ from the reference program's by a relative error of at most 0.0088.
Values sent between devices are 32-bit elements; how exact they have to be, the bound alone decides.
No kernel may reach another device: no remote copies, remote signals or barrier semaphores. Data moves between devices by JAX's collectives and lax.ppermute only.
A program may use at most 64 MiB of HBM per device.

```python
import math
from functools import partial
import jax
import jax.numpy as jnp
from jax import lax

VARS = 4
H = 128
FEAT = 12
TROW = 64
TCOL = 64
TPD = 4
LEVELS = 4
TILE_SLOTS = 16
CELLS = 262144


def tile_layout(key):
    regions = TILE_SLOTS // TPD
    half_count = regions // 2
    order_key, land_key = jax.random.split(key)
    base = jax.random.permutation(order_key, half_count).astype(jnp.int32)
    region_index = jnp.arange(regions, dtype=jnp.int32)
    device_of_region = base[region_index // 2] + region_index % 2 * half_count
    region_of_device = jnp.zeros((regions,), jnp.int32).at[device_of_region].set(region_index)
    coin = jax.random.randint(land_key, (regions, 2, 2), 0, 4)
    forced = jnp.arange(regions)[:, None, None] < 3
    ocean = (coin != 0) | forced
    number = jnp.arange(TILE_SLOTS, dtype=jnp.int32)
    device = number // TPD
    slot = number % TPD
    band_row = slot // 2
    band_column = slot % 2
    region = region_of_device[device]
    column = 2 * region + band_column
    here = ocean[region, band_row, band_column]
    width = 2 * regions

    def lattice_tile(place):
        place = place % width
        other_region = place // 2
        other_column = place % 2
        return (device_of_region[other_region] * TPD + band_row * 2 + other_column, ocean[other_region, band_row, other_column])
    west_number, west_ocean = lattice_tile(column - 1 + width)
    east_number, east_ocean = lattice_tile(column + 1)
    west = jnp.where(here & west_ocean, west_number, -1)
    east = jnp.where(here & east_ocean, east_number, -1)
    south = jnp.where((band_row == 1) & here & ocean[region, 0, band_column], band_column, -1)
    north = jnp.where((band_row == 0) & here & ocean[region, 1, band_column], 2 + band_column, -1)
    return (here, jnp.stack([west, east], axis=1).astype(jnp.int32), jnp.stack([south, north], axis=1).astype(jnp.int32), region)


def draw_level_count(key, part):
    shared = tile_layout(key)
    key = jax.random.fold_in(key, 13)
    depth_count = jax.random.randint(key, (TILE_SLOTS, TROW * TCOL), -2, LEVELS + 1)
    return jnp.where(shared[0][:, None], jnp.maximum(depth_count, 0), 0).astype(jnp.int32)


def draw_west_east(key, part):
    shared = tile_layout(key)
    key = jax.random.fold_in(key, 17)
    links = shared[1]
    closed = (jax.random.randint(key, (TILE_SLOTS,), 0, 4) == 0) & (shared[3] >= 2)
    west_link = links[:, 0]
    east_link = links[:, 1]
    east = jnp.where(closed, -1, east_link)
    west = jnp.where((west_link >= 0) & closed[jnp.maximum(west_link, 0)], -1, west_link)
    return jnp.stack([west, east], axis=1).astype(jnp.int32)


def draw_south_north(key, part):
    shared = tile_layout(key)
    key = jax.random.fold_in(key, 19)
    links = shared[2]
    closed = (jax.random.randint(key, (TILE_SLOTS,), 0, 4) == 0) & (shared[3] >= 2)
    number = jnp.arange(TILE_SLOTS, dtype=jnp.int32)
    lower = number - number % TPD + number % 2
    cut = closed[lower]
    south = jnp.where(cut, -1, links[:, 0])
    north = jnp.where(cut, -1, links[:, 1])
    return jnp.stack([south, north], axis=1).astype(jnp.int32)


def steps_of(own_key, extent, pieces, low, largest):
    factor_of = 1.0
    for dim, blocks in pieces:
        steps = jax.random.uniform(jax.random.fold_in(jax.random.fold_in(own_key, 6), dim), (blocks,), jnp.float32, low / len(pieces), largest / len(pieces))
        factor_of = factor_of * jnp.repeat(jnp.exp(steps), extent[dim] // blocks).reshape((-1,) + (1,) * (len(extent) - 1 - dim))
    return factor_of


def normal_values(stream_key, shape, spread, reach, cuts=(), kind=jnp.bfloat16):
    values = jax.random.normal(stream_key, shape, jnp.float32) * spread
    if len(cuts) > 0:
        values = steps_of(stream_key, shape, cuts, -0.22, 0.18) * values
    return jnp.clip(values, min=-reach, max=reach).astype(kind)


def setup_inputs(seed: int = 0, part: int = 0) -> dict:
    key_list = jax.random.split(jax.random.key(seed), 14)
    part_keys = jax.random.split(jax.random.fold_in(key_list[13], part), 14)
    state_init = normal_values(part_keys[0], (VARS, LEVELS, TILE_SLOTS, TROW * TCOL), 1.0, 6.0, ((1, 2), (2, 4), (3, 2)), jnp.float32)
    cotangent = normal_values(part_keys[1], (VARS, LEVELS, TILE_SLOTS, TROW * TCOL), 1.0, 6.0, ((1, 2), (2, 4), (3, 2)), jnp.float32)
    level_count = draw_level_count(jax.random.fold_in(key_list[13], 71), part)
    west_east = draw_west_east(jax.random.fold_in(key_list[13], 71), part)
    south_north = draw_south_north(jax.random.fold_in(key_list[13], 71), part)
    weight_in = normal_values(key_list[5], (H, FEAT), FEAT ** -0.5, 1.75)
    bias_in = normal_values(key_list[6], (H,), 0.5, 3.0, (), jnp.float32)
    weight_mid = normal_values(key_list[7], (H, H), H ** -0.5, 0.5)
    bias_mid = normal_values(key_list[8], (H,), 0.5, 3.0, (), jnp.float32)
    weight_out = normal_values(key_list[9], (VARS, H), H ** -0.5, 0.5)
    bias_out = normal_values(key_list[10], (VARS,), 0.5, 3.0, (), jnp.float32)
    mix_horizontal = jnp.clip(jnp.exp(jax.random.uniform(key_list[11], (VARS,), jnp.float32, math.log(0.03), math.log(0.12))), 0.03, 0.12)
    mix_vertical = jnp.clip(jnp.exp(math.log(0.25) - 1.609438 * jax.random.uniform(key_list[12], (LEVELS,), jnp.float32) ** steps_of(key_list[12], (LEVELS,), ((0, 2),), -0.2, 0.2)), 0.05, 0.25)
    return dict(state_init=state_init, cotangent=cotangent, level_count=level_count, west_east=west_east, south_north=south_north, weight_in=weight_in, bias_in=bias_in, weight_mid=weight_mid, bias_mid=bias_mid, weight_out=weight_out, bias_out=bias_out, mix_horizontal=mix_horizontal, mix_vertical=mix_vertical)


def cell_products(left, right):
    return lax.dot_general(left, right, (((1,), (1,)), ((), ())), preferred_element_type=jnp.float32)

def weight_products(weight, grad):
    return lax.dot_general(weight, grad, (((0,), (0,)), ((), ())), preferred_element_type=jnp.float32)

def closure_forward(features, weight_in, bias_in, weight_mid, bias_mid, weight_out, bias_out):
    first = jnp.tanh(jnp.dot(weight_in, features, preferred_element_type=jnp.float32) + bias_in[:, None])
    first_rounded = first.astype(jnp.bfloat16)
    second = jnp.tanh(jnp.dot(weight_mid, first_rounded, preferred_element_type=jnp.float32) + bias_mid[:, None])
    second_rounded = second.astype(jnp.bfloat16)
    output = jnp.dot(weight_out, second_rounded, preferred_element_type=jnp.float32) + bias_out[:, None]
    return (output, first, first_rounded, second, second_rounded)

def closure_backward(features, grad_out, weights):
    output, first, first_rounded, second, second_rounded = closure_forward(features, *weights)
    grad_rounded = grad_out.astype(jnp.bfloat16)
    term_weight_out = cell_products(grad_rounded, second_rounded)
    term_bias_out = lax.optimization_barrier(jnp.sum(grad_out, axis=1))
    grad_second = weight_products(weights[4], grad_rounded) * (1.0 - second * second)
    second_grad = grad_second.astype(jnp.bfloat16)
    term_weight_mid = cell_products(second_grad, first_rounded)
    term_bias_mid = lax.optimization_barrier(jnp.sum(grad_second, axis=1))
    grad_first = weight_products(weights[2], second_grad) * (1.0 - first * first)
    first_grad = grad_first.astype(jnp.bfloat16)
    term_weight_in = cell_products(first_grad, features)
    term_bias_in = lax.optimization_barrier(jnp.sum(grad_first, axis=1))
    grad_features = weight_products(weights[0], first_grad)
    return (grad_features, (term_weight_in, term_bias_in, term_weight_mid, term_bias_mid, term_weight_out, term_bias_out))

def to_blocks(array):
    return array.reshape(array.shape[0], -1, array.shape[-1]).transpose(1, 0, 2)

def from_blocks(blocks, shape):
    return blocks.transpose(1, 0, 2).reshape(shape)

def apply_closure(features, weights):
    outputs = lax.map(lambda block: closure_forward(block, *weights)[0], to_blocks(features))
    return from_blocks(outputs, (weights[4].shape[0],) + features.shape[1:])

def closure_adjoint(features, grad_out, weights):

    def visit(carried, pair):
        grad_features, terms = closure_backward(pair[0], pair[1], weights)
        return (jax.tree.map(lambda left, right: left + right, carried, terms), grad_features)
    zeros = tuple((jnp.zeros(member.shape, jnp.float32) for member in weights))
    carried, grads = lax.scan(visit, zeros, (to_blocks(features), to_blocks(grad_out)))
    return (from_blocks(grads, features.shape), carried)

def linear_parts(state, west_east, south_north):
    fields, levels, slots, cells = state.shape
    grid = state.reshape(fields, levels, slots, TROW, TCOL)
    owner = jnp.arange(slots, dtype=jnp.int32) // TPD * TPD
    south_tile = jnp.where(south_north[:, 0] >= 0, owner + south_north[:, 0], -1)
    north_tile = jnp.where(south_north[:, 1] >= 0, owner + south_north[:, 1], -1)

    def fetch(edge, tiles):
        found = jnp.take(edge, jnp.maximum(tiles, 0), axis=2)
        keep = (tiles >= 0).astype(jnp.float32)[None, None, :, None]
        return found * keep
    west_halo = fetch(grid[..., TCOL - 1], west_east[:, 0])
    east_halo = fetch(grid[..., 0], west_east[:, 1])
    south_halo = fetch(grid[:, :, :, TROW - 1, :], south_tile)
    north_halo = fetch(grid[:, :, :, 0, :], north_tile)
    east = jnp.concatenate([grid[..., 1:], east_halo[..., None]], axis=4).reshape(state.shape)
    west = jnp.concatenate([west_halo[..., None], grid[..., :-1]], axis=4).reshape(state.shape)
    north = jnp.concatenate([grid[:, :, :, 1:, :], north_halo[:, :, :, None, :]], axis=3).reshape(state.shape)
    south = jnp.concatenate([south_halo[:, :, :, None, :], grid[:, :, :, :-1, :]], axis=3).reshape(state.shape)
    zero_level = jnp.zeros_like(state[:, :1])
    above = jnp.concatenate([zero_level, state[:, :-1]], axis=1)
    below = jnp.concatenate([state[:, 1:], zero_level], axis=1)
    diffuse_h = east + west + (north + south) - 4.0 * state
    diffuse_v = above + below - 2.0 * state
    return (diffuse_h, east - west, north - south, diffuse_v)

def forward_step(state, mask, west_east, south_north, weights, mix_horizontal, mix_vertical):
    diffuse_h, across, along, diffuse_v = linear_parts(state, west_east, south_north)
    features = jnp.concatenate([state, across, along], axis=0).astype(jnp.bfloat16)
    closure = apply_closure(features, weights)
    return mask * (state + mix_horizontal[:, None, None, None] * diffuse_h + mix_vertical[None, :, None, None] * diffuse_v + closure)

def adjoint_step(state, cot, mask, west_east, south_north, weights, mix_horizontal, mix_vertical):
    grad = mask * cot
    fields = state.shape[0]
    parts, pull = jax.vjp(partial(linear_parts, west_east=west_east, south_north=south_north), state)
    features = jnp.concatenate([state, parts[1], parts[2]], axis=0).astype(jnp.bfloat16)
    grad_features, terms = closure_adjoint(features, grad, weights)
    back, = pull((mix_horizontal[:, None, None, None] * grad, grad_features[fields:2 * fields], grad_features[2 * fields:], mix_vertical[None, :, None, None] * grad))
    return (grad + grad_features[:fields] + back, terms)

def reference(state_init, cotangent, level_count, west_east, south_north, weight_in, bias_in, weight_mid, bias_mid, weight_out, bias_out, mix_horizontal, mix_vertical):
    depth_level = jnp.arange(LEVELS, dtype=jnp.int32)
    mask = (depth_level[:, None, None] < level_count[None, :, :]).astype(jnp.float32)[None]
    weights = (weight_in, bias_in, weight_mid, bias_mid, weight_out, bias_out)
    state_zero = mask * state_init
    state_one = forward_step(state_zero, mask, west_east, south_north, weights, mix_horizontal, mix_vertical)
    final_state = forward_step(state_one, mask, west_east, south_north, weights, mix_horizontal, mix_vertical)
    cot_one, late = adjoint_step(state_one, cotangent, mask, west_east, south_north, weights, mix_horizontal, mix_vertical)
    cot_zero, early = adjoint_step(state_zero, cot_one, mask, west_east, south_north, weights, mix_horizontal, mix_vertical)
    initial_cot = mask * cot_zero
    scale = 1.0 / math.sqrt(CELLS)
    grads = [(late[place] + early[place]) * scale for place in range(6)]
    return (final_state, initial_cot, grads[0], grads[1], grads[2], grads[3], grads[4], grads[5])
```

```python
import functools
import math

import jax
import jax.numpy as jnp
from jax import lax
from jax.experimental import pallas as pl
from jax.experimental.pallas import tpu as pltpu
from jax.sharding import PartitionSpec as P

TCOL = 64
LANES = 128
CHUNK = 256
BF = jnp.bfloat16
F32 = jnp.float32
VMEM_BYTES = 40 * 1024 * 1024
NT = (((1,), (1,)), ((), ()))


def dot(left, right):
    return jnp.dot(left, right, preferred_element_type=F32)


def dot_nt(left, right):
    return lax.dot_general(left, right, NT, preferred_element_type=F32)


def iota(shape, axis):
    return lax.broadcasted_iota(jnp.int32, shape, axis)


def wide(block, copies):
    return jnp.concatenate([block] * copies, axis=1)


def pack_columns(first, last):
    place = iota((8, LANES), 1) & 63
    packed = jnp.zeros((8, LANES), F32)
    for v in range(first.shape[1] // LANES):
        span = slice(v * LANES, (v + 1) * LANES)
        low = pltpu.roll(first[:, span], v, 1) if v else first[:, span]
        high = pltpu.roll(last[:, span], v + 17, 1)
        packed = jnp.where(place == v, low, packed)
        packed = jnp.where(place == 16 + v, high, packed)
    return packed


def pack_lines(first, last):
    cells = first.shape[1]
    lane = iota((8, LANES), 1)
    return jnp.where(lane < TCOL, first[:, :LANES], last[:, cells - LANES :])


def spread_columns(east_pack, west_pack, cells):
    count = cells // LANES
    east = jnp.concatenate([pltpu.roll(east_pack, 63 - v, 1) for v in range(count)], axis=1)
    west = jnp.concatenate([pltpu.roll(west_pack, 48 - v, 1) for v in range(count)], axis=1)
    return east, west


def packs_for(slot, we, sn, pools, partner, slots):
    here = lax.axis_index("tiles")
    half = lax.axis_index("sub")

    def column_pack(tile):
        safe = jnp.maximum(tile, 0)
        owner = lax.div(safe, slots)
        inside = lax.rem(safe, slots)
        where_from = jnp.bitwise_xor(here, owner)
        found = pools[0][inside]
        for k in range(1, len(pools)):
            found = jnp.where(where_from == k, pools[k][inside], found)
        return jnp.where(tile >= 0, found, 0.0)

    def line_pack(other):
        found = partner[jnp.maximum(other, 0)]
        return jnp.where(other >= 0, found, 0.0)

    west = column_pack(we[slot, 0])
    east = column_pack(we[slot, 1])
    south = line_pack(jnp.where(half == 0, sn[slot, 0], slot))
    north = line_pack(jnp.where(half == 0, slot, sn[slot, 1]))
    lane = iota((8, LANES), 1)
    lines = jnp.where(lane < TCOL, pltpu.roll(south, TCOL, 1), pltpu.roll(north, TCOL, 1))
    return east, west, lines


def halo_fields(packs, cells):
    east_pack, west_pack, lines = packs
    east, west = spread_columns(east_pack, west_pack, cells)
    return east, west, wide(lines, cells // LANES)


def places(cells):
    lane = iota((8, cells), 1)
    column = lane & (TCOL - 1)
    return column == TCOL - 1, column == 0, lane >= cells - TCOL, lane < TCOL


def neighbours(x, packs):
    cells = x.shape[1]
    east_halo, west_halo, lines = halo_fields(packs, cells)
    at_east, at_west, at_north, at_south = places(cells)
    east = jnp.where(at_east, east_halo, pltpu.roll(x, cells - 1, 1))
    west = jnp.where(at_west, west_halo, pltpu.roll(x, 1, 1))
    north = jnp.where(at_north, lines, pltpu.roll(x, cells - TCOL, 1))
    south = jnp.where(at_south, lines, pltpu.roll(x, TCOL, 1))
    return east, west, north, south


def halo_sum(packs, cells):
    east_halo, west_halo, lines = halo_fields(packs, cells)
    at_east, at_west, at_north, at_south = places(cells)
    columns = jnp.where(at_east, east_halo, jnp.where(at_west, west_halo, 0.0))
    return columns + jnp.where(at_north | at_south, lines, 0.0)


def pull_back(e_east, e_west, e_north, e_south):
    cells = e_east.shape[1]
    at_east, at_west, at_north, at_south = places(cells)
    return (
        jnp.where(at_west, 0.0, pltpu.roll(e_east, 1, 1))
        + jnp.where(at_east, 0.0, pltpu.roll(e_west, cells - 1, 1))
    ) + (
        jnp.where(at_south, 0.0, pltpu.roll(e_north, TCOL, 1))
        + jnp.where(at_north, 0.0, pltpu.roll(e_south, cells - TCOL, 1))
    )


def level_sends(even, odd):
    top = iota(even.shape, 0) < 4
    down = jnp.where(top, pltpu.roll(even, 4, 0), odd)
    up = jnp.where(top, even, pltpu.roll(odd, 4, 0))
    return down, up


def half_send(x, parity):
    top = iota(x.shape, 0) < 4
    turned = pltpu.roll(x, 4, 0)
    if parity == 0:
        return jnp.where(top, turned, 0.0), jnp.where(top, x, 0.0)
    return jnp.where(top, 0.0, x), jnp.where(top, 0.0, turned)


def level_halo(above, below, odd):
    depth = lax.axis_index("depth")
    last = lax.axis_size("depth") - 1
    above = jnp.where(depth > 0, above, 0.0)
    below = jnp.where(depth < last, below, 0.0)
    top = iota(above.shape, 0) < 4
    straight = jnp.where(top, above, below)
    turned = pltpu.roll(jnp.where(top, below, above), 4, 0)
    return jnp.where((iota(above.shape, 0) < 4) == (odd == 0), straight, turned)


def prep_kernel(mix_v, state, cot, count, x_out, g_out, mask_out, columns, lines, *sends):
    slots = state.shape[2]
    cells = state.shape[3]
    depth = lax.axis_index("depth")
    row = iota((8, cells), 0)
    level = 2 * depth + jnp.where(row < 4, 0, 1)
    mv = jnp.where(iota((8, cells), 0) < 4, mix_v[0], mix_v[1])
    for s in range(slots):
        for l in range(2):
            for f in range(4):
                r = 4 * l + f
                x_out[s, r : r + 1, :] = state[f, l, s : s + 1, :]
                g_out[s, r : r + 1, :] = cot[f, l, s : s + 1, :]
        deep = jnp.broadcast_to(count[s : s + 1, :], (8, cells))
        mask = jnp.where(level < deep, 1.0, 0.0)
        x = mask * x_out[s]
        x_out[s] = x
        g_out[s] = mask * g_out[s]
        mask_out[s] = mask
        columns[s] = pack_columns(x, x)
        lines[s] = pack_lines(x, x)
    for i in range(slots // 2):
        for kind in range(2):
            if kind == 0:
                even, odd = x_out[2 * i], x_out[2 * i + 1]
            else:
                even, odd = mv * g_out[2 * i], mv * g_out[2 * i + 1]
            down, up = level_sends(even, odd)
            if len(sends) == 1:
                sends[0][kind, i] = jnp.where(depth == 0, down, up)
            else:
                sends[0][kind, i] = down
                sends[1][kind, i] = up


def weight_kernel(
    mix_h, mix_v, bias_out, w_in, b_in, w_mid, b_mid, w_out, in_all, in_back, mid_all, mid_back,
    bias_mid, out_all, out_back, rows
):
    hidden = w_mid.shape[0]
    feature = w_in.shape[1]
    high = b_in[...].astype(BF).astype(F32)
    low = b_in[...] - high
    row = iota((32, hidden), 0)
    halves = []
    for l in range(2):
        r = iota((32, feature), 0)
        c = iota((32, feature), 1)
        chosen = (r < 24) & (((r >> 2) & 1) == l) & ((r >> 3) * 4 + (r & 3) == c)
        part = dot_nt(jnp.where(chosen, 1.0, 0.0).astype(BF), w_in[...])
        part = jnp.where(row == 24, high, jnp.where(row == 25, low, part))
        halves.append(part)
    both = jnp.concatenate(halves, axis=1)
    in_back[...] = both.astype(BF)
    padded = jnp.concatenate([both, jnp.zeros((96, 2 * hidden), F32)], axis=0)
    in_all[...] = padded.T[:, :32].astype(BF)
    middle = w_mid[...].astype(F32)
    turned = middle.T
    zero = jnp.zeros((hidden, hidden), F32)
    for source, target in ((middle, mid_all), (turned, mid_back)):
        target[...] = jnp.concatenate(
            [jnp.concatenate([source, zero], axis=1), jnp.concatenate([zero, source], axis=1)],
            axis=0,
        ).astype(BF)
    column = jnp.broadcast_to(b_mid[...], (hidden, hidden)).T
    bias_mid[...] = jnp.concatenate([column, column], axis=0)
    out = w_out[...].astype(F32)
    empty = jnp.zeros((4, hidden), F32)
    upper = jnp.concatenate([out, empty], axis=0)
    lower = jnp.concatenate([empty, out], axis=0)
    wide_out = jnp.concatenate(
        [jnp.concatenate([upper, lower], axis=1), jnp.zeros((120, 2 * hidden), F32)], axis=0
    )
    out_all[...] = wide_out[:16].astype(BF)
    out_back[...] = wide_out.T[:, :16].astype(BF)
    r8 = iota((8, LANES), 0)
    f8 = r8 & 3

    def by_field(scalars):
        return jnp.where(
            f8 == 0,
            scalars[0],
            jnp.where(f8 == 1, scalars[1], jnp.where(f8 == 2, scalars[2], scalars[3])),
        )

    rows[0] = by_field(mix_h)
    rows[1] = jnp.where(r8 < 4, mix_v[0], mix_v[1])
    rows[2] = by_field(bias_out)


def stencil(x, packs):
    east, west, north, south = neighbours(x, packs)
    diffuse = (east + west) + (north + south) - 4.0 * x
    cells = x.shape[1]
    ones = jnp.where(iota((8, cells), 0) < 2, 1.0, 0.0)
    features = jnp.concatenate([x, east - west, north - south, ones], axis=0).astype(BF)
    return diffuse, features


def write_sends(sends, kind, value, slot):
    depth = lax.axis_index("depth")

    def put(ref, part, parity):
        if parity == 0:
            ref[kind, 0] = part
        else:
            ref[kind, 0] = ref[kind, 0] + part

    for parity in range(2):

        @pl.when(lax.rem(slot, 2) == parity)
        def _():
            down, up = half_send(value, parity)
            if len(sends) == 1:
                put(sends[0], jnp.where(depth == 0, down, up), parity)
            else:
                put(sends[0], down, parity)
                put(sends[1], up, parity)


def forward_kernel(
    peers, we, sn, x_in, mask, above, below, partner, in_all, mid_all, bias_mid, out_all, rows,
    *rest
):
    pools = rest[:peers]
    x_out, first_out, second_out, feature_out, columns, lines, closure = rest[peers:]
    slot = pl.program_id(0)
    slots = pools[0].shape[0]
    x = x_in[0]
    cells = x.shape[1]
    many = cells // LANES
    packs = packs_for(slot, we, sn, pools, partner, slots)
    diffuse, features = stencil(x, packs)
    feature_out[0] = features
    bias = wide(bias_mid[...], CHUNK // LANES)
    for start in range(0, cells, CHUNK):
        span = slice(start, start + CHUNK)
        first = jnp.tanh(dot(in_all[...], feature_out[0, :, span])).astype(BF)
        first_out[0, :, span] = first
        second = jnp.tanh(dot(mid_all[...], first) + bias).astype(BF)
        second_out[0, :, span] = second
        closure[:, span] = dot(out_all[...], second)[:8]
    mh, mv, bo = (wide(rows[k], many) for k in range(3))
    vertical = pltpu.roll(x, 4, 0) + level_halo(above[0, 0], below[0, 0], lax.rem(slot, 2))
    x_new = mask[0] * (x + mh * diffuse + mv * (vertical - 2.0 * x) + (closure[...] + bo))
    x_out[0] = x_new
    columns[0] = pack_columns(x_new, x_new)
    lines[0] = pack_lines(x_new, x_new)


def backward_tail(slot, g, grad_feature, remote, rows, base, columns, lines):
    cells = g.shape[1]
    many = cells // LANES
    mh = wide(rows[0], many)
    mv = wide(rows[1], many)
    along = mh * g
    e_east = along + grad_feature[8:16]
    e_west = along - grad_feature[8:16]
    e_north = along + grad_feature[16:24]
    e_south = along - grad_feature[16:24]
    spread = mv * g
    vertical = pltpu.roll(spread, 4, 0) - 2.0 * spread
    if remote is not None:
        vertical = vertical + remote
    base[0] = (
        (g + grad_feature[0:8])
        + (pull_back(e_east, e_west, e_north, e_south) - 4.0 * along)
        + vertical
    )
    columns[0] = pack_columns(e_west, e_east)
    lines[0] = pack_lines(e_south, e_north)
    return spread


def add_terms(slot, start, second_grad, first, small, others, grad, mid, low, bias):
    hidden = mid.shape[0]
    part = dot_nt(second_grad[:hidden], first[:hidden]) + dot_nt(
        second_grad[hidden:], first[hidden:]
    )
    wings = dot_nt(small, others)
    total = grad[:, :LANES]
    for v in range(1, grad.shape[1] // LANES):
        total = total + grad[:, v * LANES : (v + 1) * LANES]

    @pl.when(slot == 0)
    def _():
        if start is None:
            mid[...] = part
            low[...] = wings
            bias[...] = total
        else:
            mid[...] = start[0][...] + part
            low[...] = start[1][...] + wings
            bias[...] = start[2][...] + total

    @pl.when(slot > 0)
    def _():
        mid[...] += part
        low[...] += wings
        bias[...] += total


def grad_rows(g):
    cells = g.shape[1]
    return jnp.concatenate([g, jnp.zeros((8, cells), F32)], axis=0).astype(BF)


def turn_kernel(
    peers, we, sn, x_in, mask, g_in, above, below, partner, in_all, mid_all, bias_mid, out_all,
    rows, out_back, mid_back, in_back, *rest
):
    pools = rest[:peers]
    (
        x_out, base, columns, lines, mid, low, bias_total,
        closure, first_all, small, trio, grad_feature,
    ) = rest[peers:]
    slot = pl.program_id(0)
    slots = pools[0].shape[0]
    x = x_in[0]
    g = g_in[0]
    cells = x.shape[1]
    many = cells // LANES
    wide2 = bias_mid.shape[0]
    packs = packs_for(slot, we, sn, pools, partner, slots)
    diffuse, features = stencil(x, packs)
    small[:32] = features
    small[32:] = grad_rows(g)
    bias = wide(bias_mid[...], CHUNK // LANES)
    for start in range(0, cells, CHUNK):
        span = slice(start, start + CHUNK)
        first = jnp.tanh(dot(in_all[...], small[:32, span]))
        first_rounded = first.astype(BF)
        first_all[:, span] = first_rounded
        second = jnp.tanh(dot(mid_all[...], first_rounded) + bias)
        second_rounded = second.astype(BF)
        trio[2 * wide2 :, span] = second_rounded
        closure[:, span] = dot(out_all[...], second_rounded)[:8]
        second_grad = dot(out_back[...], small[32:, span]) * (1.0 - second * second)
        second_grad = second_grad.astype(BF)
        trio[wide2 : 2 * wide2, span] = second_grad
        first_grad = dot(mid_back[...], second_grad) * (1.0 - first * first)
        first_grad = first_grad.astype(BF)
        trio[:wide2, span] = first_grad
        grad_feature[:, span] = dot(in_back[...], first_grad)
    add_terms(
        slot, None, trio[wide2 : 2 * wide2], first_all[...], small[...], trio[...], g, mid, low,
        bias_total,
    )
    mh, mv, bo = (wide(rows[k], many) for k in range(3))
    x_out[0] = mask[0] * (
        x + mh * diffuse + mv * (pltpu.roll(x, 4, 0) - 2.0 * x) + (closure[...] + bo)
    )
    remote = level_halo(above[0, 0], below[0, 0], lax.rem(slot, 2))
    backward_tail(slot, g, grad_feature[...], remote, rows, base, columns, lines)


def fold_terms(mid, low, bias, keep, send):
    hidden = mid.shape[0]
    top = iota((8, hidden), 0)

    def block(r, c):
        return low[8 * r : 8 * r + 8, c * hidden : (c + 1) * hidden]

    pieces = [mid[...]]
    for kind in range(3):
        pieces.append(block(kind, 0) + pltpu.roll(block(kind, 1), 4, 0))
    bias_in = block(3, 0) + block(3, 1)
    bias_mid = block(3, 2) + block(3, 3)
    pieces.append(jnp.where(top == 0, bias_in, pltpu.roll(bias_mid, 1, 0)))
    total = bias[...]
    pieces.append(
        jnp.where(
            top < 4,
            block(4, 4) + pltpu.roll(block(4, 5), 4, 0),
            total + pltpu.roll(total, 4, 0),
        )
    )
    pieces.append(jnp.zeros((8, hidden), F32))
    packed = jnp.concatenate(pieces, axis=0)
    half = packed.shape[0] // 2
    core = lax.axis_index("sub")
    keep[...] = jnp.where(core == 0, packed[:half], packed[half:])
    send[...] = jnp.where(core == 0, packed[half:], packed[:half])


def back_kernel(
    peers, we, sn, base_in, mask, x_in, partner, first_in, second_in, feature_in, rows, out_back,
    mid_back, in_back, mid_late, low_late, bias_late, *rest
):
    pools = rest[:peers]
    outs = rest[peers:]
    base, columns, lines, keep, send = outs[:5]
    sends = outs[5:-6]
    mid, low, bias_total, small, trio, grad_feature = outs[-6:]
    slot = pl.program_id(0)
    slots = pools[0].shape[0]
    cells = base_in.shape[2]
    wide2 = mid_back.shape[0]
    packs = packs_for(slot, we, sn, pools, partner, slots)
    g = mask[0] * (base_in[0] + halo_sum(packs, cells))
    small[:32] = feature_in[0]
    small[32:] = grad_rows(g)
    for start in range(0, cells, CHUNK):
        span = slice(start, start + CHUNK)
        second = second_in[0, :, span]
        first = first_in[0, :, span]
        trio[2 * wide2 :, span] = second
        second = second.astype(F32)
        first = first.astype(F32)
        second_grad = dot(out_back[...], small[32:, span]) * (1.0 - second * second)
        second_grad = second_grad.astype(BF)
        trio[wide2 : 2 * wide2, span] = second_grad
        first_grad = dot(mid_back[...], second_grad) * (1.0 - first * first)
        first_grad = first_grad.astype(BF)
        trio[:wide2, span] = first_grad
        grad_feature[:, span] = dot(in_back[...], first_grad)
    add_terms(
        slot, (mid_late, low_late, bias_late), trio[wide2 : 2 * wide2], first_in[0], small[...],
        trio[...], g, mid, low, bias_total,
    )
    spread = backward_tail(slot, g, grad_feature[...], None, rows, base, columns, lines)
    write_sends(sends, 0, x_in[0], slot)
    write_sends(sends, 1, spread, slot)

    @pl.when(slot == slots - 1)
    def _():
        fold_terms(mid, low, bias_total, keep, send)


def finish_kernel(we, sn, base_in, mask, x_in, above, below, partner, rows, *rest):
    pools = rest[:-2]
    final, initial = rest[-2:]
    slots, _, cells = base_in.shape
    many = cells // LANES
    mv = wide(rows[1], many)
    for s in range(slots):
        packs = packs_for(s, we, sn, pools, partner, slots)
        halo = level_halo(above[0, s // 2], below[0, s // 2], s % 2)
        last = x_in[s] + mask[s] * (mv * halo)
        spread = level_halo(above[1, s // 2], below[1, s // 2], s % 2)
        early = mask[s] * ((base_in[s] + spread) + halo_sum(packs, cells))
        for l in range(2):
            for f in range(4):
                r = 4 * l + f
                final[f, l, s : s + 1, :] = last[r : r + 1]
                initial[f, l, s : s + 1, :] = early[r : r + 1]


def grads_kernel(scale, low, high, w_in, b_in, w_mid, b_mid, w_out, b_out):
    hidden = w_mid.shape[0]
    packed = jnp.concatenate([low[...], high[...]], axis=0) * scale
    w_mid[...] = packed[:hidden]
    tail = packed[hidden:]
    rows = jnp.concatenate([tail[0:4], tail[8:12], tail[16:20]], axis=0)
    square = jnp.concatenate([rows, jnp.zeros((hidden - rows.shape[0], hidden), F32)], axis=0)
    w_in[...] = square.T[:, : w_in.shape[1]]
    b_in[...] = tail[24:25]
    b_mid[...] = tail[25:26]
    w_out[...] = tail[32:36]
    sums = jnp.sum(tail[36:40], axis=1, keepdims=True)
    b_out[...] = jnp.broadcast_to(sums, (4, hidden))


def vmem():
    return pl.BlockSpec(memory_space=pltpu.VMEM)


def smem():
    return pl.BlockSpec(memory_space=pltpu.SMEM)


def shape(dims, dtype=F32):
    return jax.ShapeDtypeStruct(tuple(dims), dtype)


PARAMS = pltpu.CompilerParams(vmem_limit_bytes=VMEM_BYTES)


def per_slot(dims):
    return pl.BlockSpec((1,) + tuple(dims), lambda s, we, sn: (s,) + (0,) * len(dims))


def whole(dims):
    return pl.BlockSpec(tuple(dims), lambda s, we, sn: (0,) * len(dims))


def level_block(kind, cells):
    return pl.BlockSpec((1, 1, 8, cells), lambda s, we, sn: (kind, s // 2, 0, 0))


def xor_pairs(axis, k):
    return [(i, i ^ k) for i in range(lax.axis_size(axis))]


def from_peers(packs):
    return [packs] + [
        lax.ppermute(packs, "tiles", xor_pairs("tiles", k))
        for k in range(1, lax.axis_size("tiles"))
    ]


def from_partner(lines):
    return lax.ppermute(lines, "sub", xor_pairs("sub", 1))


def from_levels(sends):
    depth = lax.axis_size("depth")
    if len(sends) == 1:
        other = lax.ppermute(sends[0], "depth", [(0, 1), (1, 0)])
        return other, other
    down = [(i, i + 1) for i in range(depth - 1)]
    return (
        lax.ppermute(sends[0], "depth", down),
        lax.ppermute(sends[1], "depth", [(j, i) for i, j in down]),
    )


def tree_sum(parts):
    while len(parts) > 1:
        parts = [parts[i] + parts[i + 1] for i in range(0, len(parts), 2)]
    return parts[0]


def sum_over(array, axis):
    return tree_sum(
        [array]
        + [lax.ppermute(array, axis, xor_pairs(axis, k)) for k in range(1, lax.axis_size(axis))]
    )


def body(
    state_init,
    cotangent,
    level_count,
    west_east,
    south_north,
    weight_in,
    bias_in,
    weight_mid,
    bias_mid,
    weight_out,
    bias_out,
    mix_horizontal,
    mix_vertical,
):
    fields, levels, slots, cells = state_init.shape
    hidden = weight_mid.shape[0]
    both = 2 * hidden
    peers = lax.axis_size("tiles")
    field = shape((slots, 8, cells))
    pack = shape((slots, 8, LANES))
    sends = [shape((2, slots // 2, 8, cells))] * (1 if lax.axis_size("depth") == 2 else 2)

    x_zero, g_late, mask, columns, lines, *levels_out = pl.pallas_call(
        prep_kernel,
        in_specs=[smem()] + [vmem()] * 3,
        out_specs=[vmem()] * (5 + len(sends)),
        out_shape=[field, field, field, pack, pack] + sends,
        compiler_params=PARAMS,
    )(mix_vertical, state_init, cotangent, level_count)
    above, below = from_levels(levels_out)
    pools = from_peers(columns)
    partner = from_partner(lines)

    in_all, in_back, mid_all, mid_back, mid_bias, out_all, out_back, rows = pl.pallas_call(
        weight_kernel,
        in_specs=[smem()] * 3 + [vmem()] * 5,
        out_specs=[vmem()] * 8,
        out_shape=[
            shape((both, 32), BF),
            shape((32, both), BF),
            shape((both, both), BF),
            shape((both, both), BF),
            shape((both, hidden)),
            shape((16, both), BF),
            shape((both, 16), BF),
            shape((3, 8, LANES)),
        ],
        compiler_params=PARAMS,
    )(
        mix_horizontal,
        mix_vertical,
        bias_out,
        weight_in,
        bias_in.reshape(1, hidden),
        weight_mid,
        bias_mid.reshape(1, hidden),
        weight_out,
    )

    one = per_slot((8, cells))
    pack_all = whole((slots, 8, LANES))
    pack_one = per_slot((8, LANES))
    forward_weights = [
        whole((both, 32)),
        whole((both, both)),
        whole((both, hidden)),
        whole((16, both)),
        whole((3, 8, LANES)),
    ]
    backward_weights = [whole((both, 16)), whole((both, both)), whole((32, both))]
    low_shape = (48, 3 * both)
    term_specs = [whole((hidden, hidden)), whole(low_shape), whole((8, LANES))]
    term_shapes = [shape((hidden, hidden)), shape(low_shape), shape((8, LANES))]

    x_one, first, second, features, columns, lines = pl.pallas_call(
        functools.partial(forward_kernel, peers),
        grid_spec=pltpu.PrefetchScalarGridSpec(
            num_scalar_prefetch=2,
            grid=(slots,),
            in_specs=[one, one, level_block(0, cells), level_block(0, cells), pack_all]
            + forward_weights
            + [pack_all] * peers,
            out_specs=[
                one,
                per_slot((both, cells)),
                per_slot((both, cells)),
                per_slot((32, cells)),
                pack_one,
                pack_one,
            ],
            scratch_shapes=[pltpu.VMEM((8, cells), F32)],
        ),
        out_shape=[
            field,
            shape((slots, both, cells), BF),
            shape((slots, both, cells), BF),
            shape((slots, 32, cells), BF),
            pack,
            pack,
        ],
        compiler_params=PARAMS,
    )(
        west_east, south_north, x_zero, mask, above, below, partner, in_all, mid_all, mid_bias,
        out_all, rows, *pools,
    )
    pools = from_peers(columns)
    partner = from_partner(lines)

    x_two, base, columns, lines, *terms = pl.pallas_call(
        functools.partial(turn_kernel, peers),
        grid_spec=pltpu.PrefetchScalarGridSpec(
            num_scalar_prefetch=2,
            grid=(slots,),
            in_specs=[one, one, one, level_block(1, cells), level_block(1, cells), pack_all]
            + forward_weights
            + backward_weights
            + [pack_all] * peers,
            out_specs=[one, one, pack_one, pack_one] + term_specs,
            scratch_shapes=[
                pltpu.VMEM((8, cells), F32),
                pltpu.VMEM((both, cells), BF),
                pltpu.VMEM((48, cells), BF),
                pltpu.VMEM((3 * both, cells), BF),
                pltpu.VMEM((32, cells), F32),
            ],
        ),
        out_shape=[field, field, pack, pack] + term_shapes,
        compiler_params=PARAMS,
    )(
        west_east, south_north, x_one, mask, g_late, above, below, partner, in_all, mid_all,
        mid_bias, out_all, rows, out_back, mid_back, in_back, *pools,
    )
    pools = from_peers(columns)
    partner = from_partner(lines)

    half = (hidden + 48) // 2
    send_block = pl.BlockSpec((2, 1, 8, cells), lambda s, we, sn: (0, s // 2, 0, 0))
    base, columns, lines, keep, give, *levels_out = pl.pallas_call(
        functools.partial(back_kernel, peers),
        grid_spec=pltpu.PrefetchScalarGridSpec(
            num_scalar_prefetch=2,
            grid=(slots,),
            in_specs=[
                one,
                one,
                one,
                pack_all,
                per_slot((both, cells)),
                per_slot((both, cells)),
                per_slot((32, cells)),
                whole((3, 8, LANES)),
            ]
            + backward_weights
            + term_specs
            + [pack_all] * peers,
            out_specs=[one, pack_one, pack_one, whole((half, hidden)), whole((half, hidden))]
            + [send_block] * len(sends),
            scratch_shapes=[
                pltpu.VMEM((hidden, hidden), F32),
                pltpu.VMEM(low_shape, F32),
                pltpu.VMEM((8, LANES), F32),
                pltpu.VMEM((48, cells), BF),
                pltpu.VMEM((3 * both, cells), BF),
                pltpu.VMEM((32, cells), F32),
            ],
        ),
        out_shape=[field, pack, pack, shape((half, hidden)), shape((half, hidden))] + sends,
        compiler_params=PARAMS,
    )(
        west_east, south_north, base, mask, x_one, partner, first, second, features, rows,
        out_back, mid_back, in_back, *terms, *pools,
    )
    total = keep + lax.ppermute(give, "sub", xor_pairs("sub", 1))
    above, below = from_levels(levels_out)
    pools = from_peers(columns)
    partner = from_partner(lines)
    total = sum_over(sum_over(total, "depth"), "tiles")

    final_state, initial_cot = pl.pallas_call(
        finish_kernel,
        in_specs=[smem(), smem()] + [vmem()] * (7 + peers),
        out_specs=[vmem()] * 2,
        out_shape=[shape(state_init.shape)] * 2,
        compiler_params=PARAMS,
    )(west_east, south_north, base, mask, x_two, above, below, partner, rows, *pools)

    other = lax.ppermute(total, "sub", xor_pairs("sub", 1))
    core = lax.axis_index("sub")
    count = (
        levels
        * lax.axis_size("depth")
        * slots
        * lax.axis_size("tiles")
        * cells
        * lax.axis_size("sub")
    )
    low = jnp.where(core == 0, total, other)
    high = jnp.where(core == 0, other, total)
    w_in, b_in, w_mid, b_mid, w_out, b_out = pl.pallas_call(
        functools.partial(grads_kernel, 1.0 / math.sqrt(count)),
        in_specs=[vmem()] * 2,
        out_specs=[vmem()] * 6,
        out_shape=[
            shape(weight_in.shape),
            shape((1, hidden)),
            shape((hidden, hidden)),
            shape((1, hidden)),
            shape(weight_out.shape),
            shape((4, hidden)),
        ],
        compiler_params=PARAMS,
    )(low, high)
    return (
        final_state,
        initial_cot,
        w_in,
        b_in.reshape(hidden),
        w_mid,
        b_mid.reshape(hidden),
        w_out,
        b_out[:, 0],
    )


def solution(mesh):
    return jax.shard_map(
        body,
        mesh=mesh,
        in_specs=(
            P("groups", "depth", "tiles", "sub"),
            P("groups", "depth", "tiles", "sub"),
            P("tiles", "sub"),
            P("tiles", None),
            P("tiles", None),
            P(),
            P(),
            P(),
            P(),
            P(),
            P(),
            P(),
            P("depth"),
        ),
        out_specs=(
            P("groups", "depth", "tiles", "sub"),
            P("groups", "depth", "tiles", "sub"),
            P("groups", None),
            P("groups"),
            P("groups", None),
            P("groups"),
            P("groups", None),
            P("groups"),
        ),
        check_vma=False,
    )
```

```python
import functools
import math

import jax
import jax.numpy as jnp
from jax import lax
from jax.experimental import pallas as pl
from jax.experimental.pallas import tpu as pltpu
from jax.sharding import PartitionSpec as P

TCOL = 64
LANES = 128
CHUNK = 2048
BF = jnp.bfloat16
F32 = jnp.float32
VMEM_BYTES = 16 * 1024 * 1024
NT = (((1,), (1,)), ((), ()))


def dot(left, right):
    return jnp.dot(left, right, preferred_element_type=F32)


def dot_nt(left, right):
    return lax.dot_general(left, right, NT, preferred_element_type=F32)


def iota(shape, axis):
    return lax.broadcasted_iota(jnp.int32, shape, axis)


def wide(block, copies):
    return jnp.concatenate([block] * copies, axis=1)


def pack_columns(first, last):
    place = iota((8, LANES), 1) & 63
    packed = jnp.zeros((8, LANES), F32)
    for v in range(first.shape[1] // LANES):
        span = slice(v * LANES, (v + 1) * LANES)
        low = pltpu.roll(first[:, span], v, 1) if v else first[:, span]
        high = pltpu.roll(last[:, span], v + 17, 1)
        packed = jnp.where(place == v, low, packed)
        packed = jnp.where(place == 16 + v, high, packed)
    return packed


def pack_lines(first, last):
    cells = first.shape[1]
    lane = iota((8, LANES), 1)
    return jnp.where(lane < TCOL, first[:, :LANES], last[:, cells - LANES :])


def halo_fields(codes, pools, partner, slots, cells):
    lane = iota((8, LANES), 1)
    count = cells // LANES
    east, west, lines = [], [], []

    def chosen(code, blocks):
        found = jnp.zeros((8, LANES), F32)
        for k, block in enumerate(blocks):
            found = jnp.where(code == k, block, found)
        return found

    column_blocks = [pool[s] for pool in pools for s in range(slots)]
    line_blocks = [partner[s] for s in range(slots)]
    for s in range(slots):
        west_pack = chosen(codes[0, s], column_blocks)
        east_pack = chosen(codes[1, s], column_blocks)
        south = pltpu.roll(chosen(codes[2, s], line_blocks), TCOL, 1)
        north = pltpu.roll(chosen(codes[3, s], line_blocks), TCOL, 1)
        east += [pltpu.roll(east_pack, 63 - v, 1) for v in range(count)]
        west += [pltpu.roll(west_pack, 48 - v, 1) for v in range(count)]
        lines += [jnp.where(lane < TCOL, south, north)] * count
    return tuple(jnp.concatenate(part, axis=1) for part in (east, west, lines))


def places(shape, cells):
    lane = iota(shape, 1) & (cells - 1)
    column = lane & (TCOL - 1)
    return column == TCOL - 1, column == 0, lane >= cells - TCOL, lane < TCOL


def neighbours(x, halos, cells):
    total = x.shape[1]
    east_halo, west_halo, lines = halos
    at_east, at_west, at_north, at_south = places(x.shape, cells)
    east = jnp.where(at_east, east_halo, pltpu.roll(x, total - 1, 1))
    west = jnp.where(at_west, west_halo, pltpu.roll(x, 1, 1))
    north = jnp.where(at_north, lines, pltpu.roll(x, total - TCOL, 1))
    south = jnp.where(at_south, lines, pltpu.roll(x, TCOL, 1))
    return east, west, north, south


def halo_sum(halos, cells):
    east_halo, west_halo, lines = halos
    at_east, at_west, at_north, at_south = places(lines.shape, cells)
    columns = jnp.where(at_east, east_halo, jnp.where(at_west, west_halo, 0.0))
    return columns + jnp.where(at_north | at_south, lines, 0.0)


def pull_back(e_east, e_west, e_north, e_south, cells):
    total = e_east.shape[1]
    at_east, at_west, at_north, at_south = places(e_east.shape, cells)
    return (
        jnp.where(at_west, 0.0, pltpu.roll(e_east, 1, 1))
        + jnp.where(at_east, 0.0, pltpu.roll(e_west, total - 1, 1))
    ) + (
        jnp.where(at_south, 0.0, pltpu.roll(e_north, TCOL, 1))
        + jnp.where(at_north, 0.0, pltpu.roll(e_south, total - TCOL, 1))
    )


def write_edges(columns, lines, first_column, last_column, first_line, last_line):
    slots = columns.shape[0]
    cells = first_column.shape[1] // slots
    for s in range(slots):
        span = slice(s * cells, (s + 1) * cells)
        columns[s] = pack_columns(first_column[:, span], last_column[:, span])
        lines[s] = pack_lines(first_line[:, span], last_line[:, span])


def write_sends(sends, kind, x, cells):
    depth = lax.axis_index("depth")
    top = iota((8, cells), 0) < 4
    for i in range(x.shape[1] // (2 * cells)):
        even = x[:, 2 * i * cells : (2 * i + 1) * cells]
        odd = x[:, (2 * i + 1) * cells : (2 * i + 2) * cells]
        down = jnp.where(top, pltpu.roll(even, 4, 0), odd)
        up = jnp.where(top, even, pltpu.roll(odd, 4, 0))
        if len(sends) == 1:
            sends[0][kind, i] = jnp.where(depth == 0, down, up)
        else:
            sends[0][kind, i] = down
            sends[1][kind, i] = up


def level_halo(above_ref, below_ref, kind):
    depth = lax.axis_index("depth")
    last = lax.axis_size("depth") - 1
    parts = []
    for i in range(above_ref.shape[1]):
        above = jnp.where(depth > 0, above_ref[kind, i], 0.0)
        below = jnp.where(depth < last, below_ref[kind, i], 0.0)
        top = iota(above.shape, 0) < 4
        parts.append(jnp.where(top, above, pltpu.roll(below, 4, 0)))
        parts.append(jnp.where(top, pltpu.roll(above, 4, 0), below))
    return jnp.concatenate(parts, axis=1)


def fetch(pairs, sems):
    copies = [
        pltpu.make_async_copy(source, target, sems.at[i])
        for i, (source, target) in enumerate(pairs)
    ]
    for copy in copies:
        copy.start()
    for copy in copies:
        copy.wait()


def prep_kernel(sent, mix_v_in, state_in, cot_in, count_in, *rest):
    x_out, g_out, mask_out, columns, lines = rest[:5]
    sends = rest[5 : 5 + sent]
    mix_v, state, cot, count, sems = rest[5 + sent :]
    fetch(
        [(mix_v_in, mix_v), (count_in, count), (state_in, state), (cot_in, cot)], sems
    )
    slots = state.shape[2]
    cells = state.shape[3]
    depth = lax.axis_index("depth")
    for s in range(slots):
        span = slice(s * cells, (s + 1) * cells)
        for l in range(2):
            for f in range(4):
                r = 4 * l + f
                x_out[r : r + 1, span] = state[f, l, s : s + 1, :]
                g_out[r : r + 1, span] = cot[f, l, s : s + 1, :]
    deep = jnp.concatenate(
        [jnp.broadcast_to(count[s : s + 1, :], (8, cells)) for s in range(slots)], axis=1
    )
    upper = iota(deep.shape, 0) < 4
    mask = jnp.where(2 * depth + jnp.where(upper, 0, 1) < deep, 1.0, 0.0)
    x = mask * x_out[...]
    g = mask * g_out[...]
    mask_out[...] = mask
    x_out[...] = x
    g_out[...] = g
    write_edges(columns, lines, x, x, x, x)
    write_sends(sends, 0, x, cells)
    write_sends(sends, 1, jnp.where(upper, mix_v[0], mix_v[1]) * g, cells)


def weight_kernel(
    mix_h_in, mix_v_in, bias_out_in, we_in, sn_in, w_in_in, b_in_in, w_mid_in, b_mid_in, w_out_in,
    in_all, in_back, mid_all, mid_back, bias_mid, out_all, out_back, rows, codes,
    mix_h, mix_v, bias_out, we, sn, w_in, b_in, w_mid, b_mid, w_out, sems
):
    fetch(
        [
            (mix_h_in, mix_h), (mix_v_in, mix_v), (bias_out_in, bias_out), (we_in, we),
            (sn_in, sn), (w_in_in, w_in), (b_in_in, b_in), (w_mid_in, w_mid), (b_mid_in, b_mid),
            (w_out_in, w_out),
        ],
        sems,
    )
    hidden = w_mid.shape[0]
    feature = w_in.shape[0]
    high = b_in[...].astype(BF).astype(F32)
    low = b_in[...] - high
    row = iota((32, hidden), 0)
    halves = []
    for l in range(2):
        r = iota((32, feature), 0)
        c = iota((32, feature), 1)
        chosen = (r < 24) & (((r >> 2) & 1) == l) & ((r >> 3) * 4 + (r & 3) == c)
        part = dot(jnp.where(chosen, 1.0, 0.0).astype(BF), w_in[...])
        part = jnp.where(row == 24, high, jnp.where(row == 25, low, part))
        halves.append(part)
    both = jnp.concatenate(halves, axis=1)
    in_back[...] = both.astype(BF)
    padded = jnp.concatenate([both, jnp.zeros((96, 2 * hidden), F32)], axis=0)
    in_all[...] = padded.T[:, :32].astype(BF)
    middle = w_mid[...].astype(F32)
    turned = middle.T
    zero = jnp.zeros((hidden, hidden), F32)
    for source, target in ((middle, mid_all), (turned, mid_back)):
        target[...] = jnp.concatenate(
            [jnp.concatenate([source, zero], axis=1), jnp.concatenate([zero, source], axis=1)],
            axis=0,
        ).astype(BF)
    column = jnp.broadcast_to(b_mid[...], (hidden, hidden)).T
    bias_mid[...] = jnp.concatenate([column, column], axis=0)
    out = w_out[...].astype(F32)
    empty = jnp.zeros((4, hidden), F32)
    upper = jnp.concatenate([out, empty], axis=0)
    lower = jnp.concatenate([empty, out], axis=0)
    wide_out = jnp.concatenate(
        [jnp.concatenate([upper, lower], axis=1), jnp.zeros((120, 2 * hidden), F32)], axis=0
    )
    out_all[...] = wide_out[:16].astype(BF)
    out_back[...] = wide_out.T[:, :16].astype(BF)
    r8 = iota((8, LANES), 0)
    f8 = r8 & 3

    def by_field(scalars):
        return jnp.where(
            f8 == 0,
            scalars[0],
            jnp.where(f8 == 1, scalars[1], jnp.where(f8 == 2, scalars[2], scalars[3])),
        )

    rows[0] = by_field(mix_h)
    rows[1] = jnp.where(r8 < 4, mix_v[0], mix_v[1])
    rows[2] = by_field(bias_out)
    here = lax.axis_index("tiles")
    half = lax.axis_index("sub")
    slots = codes.shape[1]
    for s in range(slots):
        for side in range(2):
            tile = we[side, s]
            safe = jnp.maximum(tile, 0)
            owner = jnp.bitwise_xor(lax.div(safe, slots), here)
            code = jnp.where(tile >= 0, owner * slots + lax.rem(safe, slots), -1)
            codes[side, s] = jnp.full((8, LANES), code, jnp.int32)
            code = jnp.where(half == side, sn[side, s], s)
            codes[2 + side, s] = jnp.full((8, LANES), code, jnp.int32)


def stencil(x, halos, cells):
    east, west, north, south = neighbours(x, halos, cells)
    diffuse = (east + west) + (north + south) - 4.0 * x
    ones = jnp.where(iota(x.shape, 0) < 2, 1.0, 0.0)
    features = jnp.concatenate([x, east - west, north - south, ones], axis=0).astype(BF)
    return diffuse, features


def keep_first(first_out, span, first):
    hidden = first.shape[0] // 2
    ones = jnp.ones((16, first.shape[1]), BF)
    for l in range(2):
        base = l * (hidden + 16)
        first_out[base : base + hidden, span] = first[l * hidden : (l + 1) * hidden]
        first_out[base + hidden : base + hidden + 16, span] = ones


def forward_kernel(
    peers, x_in, mask, above, below, partner, codes, in_all, mid_all, bias_mid, out_all, rows,
    *rest
):
    pools = rest[:peers]
    x_out, first_out, second_out, feature_out, columns, lines, closure = rest[peers:]
    slots = partner.shape[0]
    x = x_in[...]
    total = x.shape[1]
    cells = total // slots
    halos = halo_fields(codes, pools, partner, slots, cells)
    diffuse, features = stencil(x, halos, cells)
    feature_out[...] = features
    bias = wide(bias_mid[...], CHUNK // LANES)
    for start in range(0, total, CHUNK):
        span = slice(start, start + CHUNK)
        first = jnp.tanh(dot(in_all[...], feature_out[:, span])).astype(BF)
        keep_first(first_out, span, first)
        second = jnp.tanh(dot(mid_all[...], first) + bias).astype(BF)
        second_out[:, span] = second
        closure[:, span] = dot(out_all[...], second)[:8]
    mh, mv, bo = (wide(rows[k], total // LANES) for k in range(3))
    vertical = pltpu.roll(x, 4, 0) + level_halo(above, below, 0)
    x_new = mask[...] * (x + mh * diffuse + mv * (vertical - 2.0 * x) + (closure[...] + bo))
    x_out[...] = x_new
    write_edges(columns, lines, x_new, x_new, x_new, x_new)


def backward_tail(g, grad_feature, remote, rows, base, columns, lines, g_sum):
    total = g.shape[1]
    many = total // LANES
    cells = total // columns.shape[0]
    mh = wide(rows[0], many)
    mv = wide(rows[1], many)
    along = mh * g
    e_east = along + grad_feature[8:16]
    e_west = along - grad_feature[8:16]
    e_north = along + grad_feature[16:24]
    e_south = along - grad_feature[16:24]
    spread = mv * g
    vertical = pltpu.roll(spread, 4, 0) - 2.0 * spread
    if remote is not None:
        vertical = vertical + remote
    write_edges(columns, lines, e_west, e_east, e_south, e_north)
    base[...] = (
        (g + grad_feature[0:8])
        + (pull_back(e_east, e_west, e_north, e_south, cells) - 4.0 * along)
        + vertical
    )
    sums = [g[:, v * LANES : (v + 1) * LANES] for v in range(many)]
    g_sum[...] = tree_sum(sums)
    return spread


def grad_rows(g):
    return jnp.concatenate([g, jnp.zeros(g.shape, F32)], axis=0).astype(BF)


def turn_kernel(
    peers, x_in, mask, g_in, above, below, partner, codes, in_all, mid_all, bias_mid, out_all,
    rows, out_back, mid_back, in_back, *rest
):
    pools = rest[:peers]
    (
        x_out, base, columns, lines, g_sum, first_out, second_out, feature_out, grad_out,
        second_grad_out, first_grad_out, closure, grad_feature,
    ) = rest[peers:]
    slots = partner.shape[0]
    x = x_in[...]
    g = g_in[...]
    total = x.shape[1]
    cells = total // slots
    halos = halo_fields(codes, pools, partner, slots, cells)
    diffuse, features = stencil(x, halos, cells)
    feature_out[...] = features
    grad_out[...] = grad_rows(g)
    bias = wide(bias_mid[...], CHUNK // LANES)
    for start in range(0, total, CHUNK):
        span = slice(start, start + CHUNK)
        first = jnp.tanh(dot(in_all[...], feature_out[:, span])).astype(BF)
        keep_first(first_out, span, first)
        second = jnp.tanh(dot(mid_all[...], first) + bias).astype(BF)
        second_out[:, span] = second
        closure[:, span] = dot(out_all[...], second)[:8]
        second_grad = times_slope(dot(out_back[...], grad_out[:, span]), second)
        second_grad_out[:, span] = second_grad
        first_grad = times_slope(dot(mid_back[...], second_grad), first)
        first_grad_out[:, span] = first_grad
        grad_feature[:, span] = dot(in_back[...], first_grad)
    remote = level_halo(above, below, 1)
    backward_tail(g, grad_feature[...], remote, rows, base, columns, lines, g_sum)
    mh, mv, bo = (wide(rows[k], total // LANES) for k in range(3))
    x_out[...] = mask[...] * (
        x + mh * diffuse + mv * (pltpu.roll(x, 4, 0) - 2.0 * x) + (closure[...] + bo)
    )


def times_slope(grad, value):
    return grad.astype(BF) * (1.0 - value * value)


def back_kernel(
    peers, base_in, mask, x_in, partner, codes, first_in, second_in, rows, out_back, mid_back,
    in_back, *rest
):
    pools = rest[:peers]
    base, columns, lines, g_sum, grad_out, second_grad_out, first_grad_out = rest[
        peers : peers + 7
    ]
    sends = rest[peers + 7 : -1]
    grad_feature = rest[-1]
    slots = partner.shape[0]
    total = base_in.shape[1]
    cells = total // slots
    hidden = mid_back.shape[0] // 2
    halos = halo_fields(codes, pools, partner, slots, cells)
    g = mask[...] * (base_in[...] + halo_sum(halos, cells))
    grad_out[...] = grad_rows(g)
    for start in range(0, total, CHUNK):
        span = slice(start, start + CHUNK)
        first = jnp.concatenate(
            [first_in[:hidden, span], first_in[hidden + 16 : 2 * hidden + 16, span]], axis=0
        )
        second_grad = times_slope(dot(out_back[...], grad_out[:, span]), second_in[:, span])
        second_grad_out[:, span] = second_grad
        first_grad = times_slope(dot(mid_back[...], second_grad), first)
        first_grad_out[:, span] = first_grad
        grad_feature[:, span] = dot(in_back[...], first_grad)
    spread = backward_tail(g, grad_feature[...], None, rows, base, columns, lines, g_sum)
    write_sends(sends, 0, x_in[...], cells)
    write_sends(sends, 1, spread, cells)


def term_sums(first, second, features, grad, second_grad, first_grad):
    hidden = first.shape[0] // 2 - 16
    side = hidden + 16
    mid = dot_nt(second_grad[:hidden], first[:side]) + dot_nt(second_grad[hidden:], first[side:])
    return mid, dot_nt(first_grad[...], features[...]), dot_nt(second[...], grad[...])


def late_terms_kernel(*refs):
    for value, out in zip(term_sums(*refs[:6]), refs[6:]):
        out[...] = value


def early_terms_kernel(*refs):
    late = refs[6:10]
    g_sum, keep, send = refs[10:]
    mid, wing, out = (a + b[...] for a, b in zip(term_sums(*refs[:6]), late[:3]))
    total = late[3][...] + g_sum[...]
    hidden = mid.shape[0]
    top = iota((8, hidden), 0)

    def turned(block):
        blank = jnp.zeros((block.shape[0], hidden - block.shape[1]), F32)
        return jnp.concatenate([block, blank], axis=1).T

    low, high = turned(wing[:hidden]), turned(wing[hidden:])
    pieces = [mid[:, :hidden]]
    for kind in range(3):
        span = slice(8 * kind, 8 * kind + 8)
        pieces.append(low[span] + pltpu.roll(high[span], 4, 0))
    bias_in = low[24:32] + high[24:32]
    bias_mid = turned(mid[:, hidden:])[:8]
    pieces.append(jnp.where(top == 0, bias_in, pltpu.roll(bias_mid, 1, 0)))
    low, high = turned(out[:hidden]), turned(out[hidden:])
    pieces.append(
        jnp.where(top < 4, low[:8] + pltpu.roll(high[:8], 4, 0), total + pltpu.roll(total, 4, 0))
    )
    pieces.append(jnp.zeros((8, hidden), F32))
    packed = jnp.concatenate(pieces, axis=0)
    half = packed.shape[0] // 2
    core = lax.axis_index("sub")
    keep[...] = jnp.where(core == 0, packed[:half], packed[half:])
    send[...] = jnp.where(core == 0, packed[half:], packed[:half])


def finish_kernel(base_in, mask, x_in, above, below, partner, codes, rows, *rest):
    pools = rest[:-2]
    final, initial = rest[-2:]
    slots = partner.shape[0]
    total = base_in.shape[1]
    cells = total // slots
    mv = wide(rows[1], total // LANES)
    halos = halo_fields(codes, pools, partner, slots, cells)
    last = x_in[...] + mask[...] * (mv * level_halo(above, below, 0))
    early = mask[...] * ((base_in[...] + level_halo(above, below, 1)) + halo_sum(halos, cells))
    for s in range(slots):
        span = slice(s * cells, (s + 1) * cells)
        for l in range(2):
            for f in range(4):
                r = 4 * l + f
                final[f, l, s : s + 1, :] = last[r : r + 1, span]
                initial[f, l, s : s + 1, :] = early[r : r + 1, span]


def grads_kernel(scale, mine, other, w_in, b_in, w_mid, b_mid, w_out, b_out):
    hidden = w_mid.shape[0]
    core = lax.axis_index("sub")
    low = jnp.where(core == 0, mine[...], other[...])
    high = jnp.where(core == 0, other[...], mine[...])
    packed = jnp.concatenate([low, high], axis=0) * scale
    w_mid[...] = packed[:hidden]
    tail = packed[hidden:]
    w_in[0:4] = tail[0:4]
    w_in[4:8] = tail[8:12]
    w_in[8:12] = tail[16:20]
    b_in[...] = tail[24:25]
    b_mid[...] = tail[25:26]
    w_out[...] = tail[32:36]
    sums = jnp.broadcast_to(jnp.sum(tail[36:40], axis=1, keepdims=True), (4, hidden))
    spot = iota((4, hidden), 0) == iota((4, hidden), 1)
    b_out[...] = jnp.sum(jnp.where(spot, sums, 0.0), axis=0, keepdims=True)


def call(kernel, inputs, outs, scratch=(), spaces=None):
    return pl.pallas_call(
        kernel,
        in_specs=[pl.BlockSpec(memory_space=spaces or pltpu.VMEM)] * len(inputs),
        out_specs=[pl.BlockSpec(memory_space=pltpu.VMEM)] * len(outs),
        out_shape=outs,
        scratch_shapes=list(scratch),
        compiler_params=pltpu.CompilerParams(vmem_limit_bytes=VMEM_BYTES),
    )(*(inputs if spaces is None else [pltpu.with_memory_space_constraint(a, spaces) for a in inputs]))


def shape(dims, dtype=F32):
    return jax.ShapeDtypeStruct(tuple(dims), dtype)


def xor_pairs(axis, k):
    return [(i, i ^ k) for i in range(lax.axis_size(axis))]


def from_peers(packs):
    return [packs] + [
        lax.ppermute(packs, "tiles", xor_pairs("tiles", k))
        for k in range(1, lax.axis_size("tiles"))
    ]


def from_partner(lines):
    return lax.ppermute(lines, "sub", xor_pairs("sub", 1))


def from_levels(sends):
    depth = lax.axis_size("depth")
    if len(sends) == 1:
        other = lax.ppermute(sends[0], "depth", [(0, 1), (1, 0)])
        return other, other
    down = [(i, i + 1) for i in range(depth - 1)]
    return (
        lax.ppermute(sends[0], "depth", down),
        lax.ppermute(sends[1], "depth", [(j, i) for i, j in down]),
    )


def tree_sum(parts):
    while len(parts) > 1:
        parts = [parts[i] + parts[i + 1] for i in range(0, len(parts), 2)]
    return parts[0]


def sum_over(array, axis):
    return tree_sum(
        [array]
        + [lax.ppermute(array, axis, xor_pairs(axis, k)) for k in range(1, lax.axis_size(axis))]
    )


def body(
    state_init,
    cotangent,
    level_count,
    west_east,
    south_north,
    weight_in,
    bias_in,
    weight_mid,
    bias_mid,
    weight_out,
    bias_out,
    mix_horizontal,
    mix_vertical,
):
    fields, levels, slots, cells = state_init.shape
    hidden = weight_mid.shape[0]
    both = 2 * hidden
    total = slots * cells
    peers = lax.axis_size("tiles")
    field = shape((8, total))
    pack = shape((slots, 8, LANES))
    sends = [shape((2, slots // 2, 8, cells))] * (1 if lax.axis_size("depth") == 2 else 2)
    hidden_rows = shape((both, total), BF)
    first_rows = shape((both + 32, total), BF)
    vmem, smem = pltpu.VMEM, pltpu.SMEM

    inputs = [mix_vertical, state_init, cotangent, level_count]
    x_zero, g_late, mask, columns, lines, *levels_out = call(
        functools.partial(prep_kernel, len(sends)),
        inputs,
        [field, field, field, pack, pack] + sends,
        [
            smem(mix_vertical.shape, F32),
            vmem(state_init.shape, F32),
            vmem(cotangent.shape, F32),
            vmem(level_count.shape, jnp.int32),
            pltpu.SemaphoreType.DMA((len(inputs),)),
        ],
        pltpu.HBM,
    )
    above, below = from_levels(levels_out)
    pools = from_peers(columns)
    partner = from_partner(lines)

    inputs = [
        mix_horizontal,
        mix_vertical,
        bias_out,
        west_east.T,
        south_north.T,
        weight_in.T,
        bias_in.reshape(1, hidden),
        weight_mid,
        bias_mid.reshape(1, hidden),
        weight_out,
    ]
    in_all, in_back, mid_all, mid_back, mid_bias, out_all, out_back, rows, codes = call(
        weight_kernel,
        inputs,
        [
            shape((both, 32), BF),
            shape((32, both), BF),
            shape((both, both), BF),
            shape((both, both), BF),
            shape((both, hidden)),
            shape((16, both), BF),
            shape((both, 16), BF),
            shape((3, 8, LANES)),
            shape((4, slots, 8, LANES), jnp.int32),
        ],
        [(smem if i < 5 else vmem)(a.shape, a.dtype) for i, a in enumerate(inputs)]
        + [pltpu.SemaphoreType.DMA((len(inputs),))],
        pltpu.HBM,
    )
    forward_weights = [in_all, mid_all, mid_bias, out_all, rows]
    backward_weights = [out_back, mid_back, in_back]

    x_one, first, second, features, columns, lines = call(
        functools.partial(forward_kernel, peers),
        [x_zero, mask, above, below, partner, codes] + forward_weights + pools,
        [field, first_rows, hidden_rows, shape((32, total), BF), pack, pack],
        [vmem((8, total), F32)],
    )
    pools = from_peers(columns)
    partner = from_partner(lines)

    x_two, base, columns, lines, late_sum, *late = call(
        functools.partial(turn_kernel, peers),
        [x_one, mask, g_late, above, below, partner, codes]
        + forward_weights
        + backward_weights
        + pools,
        [
            field, field, pack, pack, shape((8, LANES)), first_rows, hidden_rows,
            shape((32, total), BF), shape((16, total), BF), hidden_rows, hidden_rows,
        ],
        [vmem((8, total), F32), vmem((32, total), F32)],
    )
    pools = from_peers(columns)
    partner = from_partner(lines)
    late = call(
        late_terms_kernel,
        late,
        [shape((hidden, hidden + 16)), shape((both, 32)), shape((both, 16))],
    )

    base, columns, lines, early_sum, grad, second_grad, first_grad, *levels_out = call(
        functools.partial(back_kernel, peers),
        [base, mask, x_one, partner, codes, first, second, rows] + backward_weights + pools,
        [
            field, pack, pack, shape((8, LANES)), shape((16, total), BF), hidden_rows, hidden_rows,
        ]
        + sends,
        [vmem((32, total), F32)],
    )
    above, below = from_levels(levels_out)
    pools = from_peers(columns)
    partner = from_partner(lines)
    half = shape(((hidden + 48) // 2, hidden))
    keep, give = call(
        early_terms_kernel,
        [first, second, features, grad, second_grad, first_grad, *late, late_sum, early_sum],
        [half, half],
    )
    terms = keep + lax.ppermute(give, "sub", xor_pairs("sub", 1))
    terms = sum_over(sum_over(terms, "depth"), "tiles")
    final_state, initial_cot = call(
        finish_kernel,
        [base, mask, x_two, above, below, partner, codes, rows] + pools,
        [shape(state_init.shape)] * 2,
    )
    count = (
        levels
        * lax.axis_size("depth")
        * slots
        * lax.axis_size("tiles")
        * cells
        * lax.axis_size("sub")
    )
    w_in, b_in, w_mid, b_mid, w_out, b_out = call(
        functools.partial(grads_kernel, 1.0 / math.sqrt(count)),
        [terms, lax.ppermute(terms, "sub", xor_pairs("sub", 1))],
        [
            shape(weight_in.T.shape),
            shape((1, hidden)),
            shape((hidden, hidden)),
            shape((1, hidden)),
            shape(weight_out.shape),
            shape((1, hidden)),
        ],
    )
    return (
        final_state,
        initial_cot,
        w_in.T,
        b_in.reshape(hidden),
        w_mid,
        b_mid.reshape(hidden),
        w_out,
        b_out[0, :fields],
    )


def solution(mesh):
    return jax.shard_map(
        body,
        mesh=mesh,
        in_specs=(
            P("groups", "depth", "tiles", "sub"),
            P("groups", "depth", "tiles", "sub"),
            P("tiles", "sub"),
            P("tiles", None),
            P("tiles", None),
            P(),
            P(),
            P(),
            P(),
            P(),
            P(),
            P(),
            P("depth"),
        ),
        out_specs=(
            P("groups", "depth", "tiles", "sub"),
            P("groups", "depth", "tiles", "sub"),
            P("groups", None),
            P("groups"),
            P("groups", None),
            P("groups"),
            P("groups", None),
            P("groups"),
        ),
        check_vma=False,
    )
```

```python
import functools
import math

import jax
import jax.numpy as jnp
from jax import lax
from jax.experimental import pallas as pl
from jax.experimental.pallas import tpu as pltpu
from jax.sharding import PartitionSpec as P

TCOL = 64
LANES = 128
CHUNK = 2048
BF = jnp.bfloat16
F32 = jnp.float32
VMEM_BYTES = 16 * 1024 * 1024
NT = (((1,), (1,)), ((), ()))


def dot(left, right):
    return jnp.dot(left, right, preferred_element_type=F32)


def dot_nt(left, right):
    return lax.dot_general(left, right, NT, preferred_element_type=F32)


def iota(shape, axis):
    return lax.broadcasted_iota(jnp.int32, shape, axis)


def wide(block, copies):
    return jnp.concatenate([block] * copies, axis=1)


def pack_columns(first, last, place_of_slot):
    place = iota((8, LANES), 1) & 63
    packed = jnp.zeros((8, LANES), F32)
    for v in range(first.shape[1] // LANES):
        span = slice(v * LANES, (v + 1) * LANES)
        at = v + place_of_slot
        low = pltpu.roll(first[:, span], at, 1) if at else first[:, span]
        high = pltpu.roll(last[:, span], at + 17, 1)
        packed = jnp.where(place == at, low, packed)
        packed = jnp.where(place == at + 16, high, packed)
    return packed


def pack_lines(first, last):
    cells = first.shape[1]
    lane = iota((8, LANES), 1)
    return jnp.where(lane < TCOL, first[:, :LANES], last[:, cells - LANES :])


def halo_fields(codes, pools, partner, slots, cells, skip=None):
    lane = iota((8, LANES), 1)
    count = cells // LANES
    east, west, lines = [], [], []

    def chosen(code, blocks):
        found = jnp.zeros((8, LANES), F32)
        for k, block in enumerate(blocks):
            found = jnp.where(code == k, block, found)
        return found

    column_blocks = []
    for pool in pools:
        for i in range(slots // 2):
            both = pool[i] if skip is None else pool[skip + 8 * i : skip + 8 * i + 8]
            column_blocks += [both, pltpu.roll(both, LANES - 32, 1)]
    line_blocks = [partner[s] for s in range(slots)]
    for s in range(slots):
        west_pack = chosen(codes[0, s], column_blocks)
        east_pack = chosen(codes[1, s], column_blocks)
        south = pltpu.roll(chosen(codes[2, s], line_blocks), TCOL, 1)
        north = pltpu.roll(chosen(codes[3, s], line_blocks), TCOL, 1)
        east += [pltpu.roll(east_pack, 63 - v, 1) for v in range(count)]
        west += [pltpu.roll(west_pack, 48 - v, 1) for v in range(count)]
        lines += [jnp.where(lane < TCOL, south, north)] * count
    return tuple(jnp.concatenate(part, axis=1) for part in (east, west, lines))


def places(shape, cells):
    lane = iota(shape, 1) & (cells - 1)
    column = lane & (TCOL - 1)
    return column == TCOL - 1, column == 0, lane >= cells - TCOL, lane < TCOL


def neighbours(x, halos, cells):
    total = x.shape[1]
    east_halo, west_halo, lines = halos
    at_east, at_west, at_north, at_south = places(x.shape, cells)
    east = jnp.where(at_east, east_halo, pltpu.roll(x, total - 1, 1))
    west = jnp.where(at_west, west_halo, pltpu.roll(x, 1, 1))
    north = jnp.where(at_north, lines, pltpu.roll(x, total - TCOL, 1))
    south = jnp.where(at_south, lines, pltpu.roll(x, TCOL, 1))
    return east, west, north, south


def halo_sum(halos, cells):
    east_halo, west_halo, lines = halos
    at_east, at_west, at_north, at_south = places(lines.shape, cells)
    columns = jnp.where(at_east, east_halo, jnp.where(at_west, west_halo, 0.0))
    return columns + jnp.where(at_north | at_south, lines, 0.0)


def pull_back(e_east, e_west, e_north, e_south, cells):
    total = e_east.shape[1]
    at_east, at_west, at_north, at_south = places(e_east.shape, cells)
    return (
        jnp.where(at_west, 0.0, pltpu.roll(e_east, 1, 1))
        + jnp.where(at_east, 0.0, pltpu.roll(e_west, total - 1, 1))
    ) + (
        jnp.where(at_south, 0.0, pltpu.roll(e_north, TCOL, 1))
        + jnp.where(at_north, 0.0, pltpu.roll(e_south, total - TCOL, 1))
    )


def write_edges(columns, lines, first_column, last_column, first_line, last_line):
    slots = lines.shape[0]
    cells = first_column.shape[1] // slots
    spans = [slice(s * cells, (s + 1) * cells) for s in range(slots)]
    packs = [
        pack_columns(first_column[:, span], last_column[:, span], 32 * (s % 2))
        for s, span in enumerate(spans)
    ]
    for s, span in enumerate(spans):
        if s % 2 == 0:
            columns[s // 2] = packs[s] + packs[s + 1]
        lines[s] = pack_lines(first_line[:, span], last_line[:, span])


def write_sends(sends, kind, x, cells):
    depth = lax.axis_index("depth")
    top = iota((8, cells), 0) < 4
    for i in range(x.shape[1] // (2 * cells)):
        even = x[:, 2 * i * cells : (2 * i + 1) * cells]
        odd = x[:, (2 * i + 1) * cells : (2 * i + 2) * cells]
        down = jnp.where(top, pltpu.roll(even, 4, 0), odd)
        up = jnp.where(top, even, pltpu.roll(odd, 4, 0))
        if len(sends) == 1:
            sends[0][kind, i] = jnp.where(depth == 0, down, up)
        else:
            sends[0][kind, i] = down
            sends[1][kind, i] = up


def level_halo(above_ref, below_ref, kind):
    depth = lax.axis_index("depth")
    last = lax.axis_size("depth") - 1
    parts = []
    for i in range(above_ref.shape[1]):
        above = jnp.where(depth > 0, above_ref[kind, i], 0.0)
        below = jnp.where(depth < last, below_ref[kind, i], 0.0)
        top = iota(above.shape, 0) < 4
        parts.append(jnp.where(top, above, pltpu.roll(below, 4, 0)))
        parts.append(jnp.where(top, pltpu.roll(above, 4, 0), below))
    return jnp.concatenate(parts, axis=1)


def fetch(pairs, sems):
    copies = [
        pltpu.make_async_copy(source, target, sems.at[i])
        for i, (source, target) in enumerate(pairs)
    ]
    for copy in copies:
        copy.start()
    for copy in copies:
        copy.wait()


def prep_kernel(sent, mix_v_in, state_in, cot_in, count_in, *rest):
    x_out, g_out, mask_out, columns, lines = rest[:5]
    sends = rest[5 : 5 + sent]
    mix_v, state, cot, count, sems = rest[5 + sent :]
    fetch(
        [(mix_v_in, mix_v), (count_in, count), (state_in, state), (cot_in, cot)], sems
    )
    slots = state.shape[2]
    cells = state.shape[3]
    depth = lax.axis_index("depth")
    for s in range(slots):
        span = slice(s * cells, (s + 1) * cells)
        for l in range(2):
            for f in range(4):
                r = 4 * l + f
                x_out[r : r + 1, span] = state[f, l, s : s + 1, :]
                g_out[r : r + 1, span] = cot[f, l, s : s + 1, :]
    deep = jnp.concatenate(
        [jnp.broadcast_to(count[s : s + 1, :], (8, cells)) for s in range(slots)], axis=1
    )
    upper = iota(deep.shape, 0) < 4
    mask = jnp.where(2 * depth + jnp.where(upper, 0, 1) < deep, 1.0, 0.0)
    x = mask * x_out[...]
    g = mask * g_out[...]
    mask_out[...] = mask
    x_out[...] = x
    g_out[...] = g
    write_edges(columns, lines, x, x, x, x)
    write_sends(sends, 0, x, cells)
    write_sends(sends, 1, jnp.where(upper, mix_v[0], mix_v[1]) * g, cells)


def weight_kernel(
    mix_h_in, mix_v_in, bias_out_in, we_in, sn_in, w_in_in, b_in_in, w_mid_in, b_mid_in, w_out_in,
    in_all, in_back, mid_all, mid_back, bias_mid, out_all, out_back, rows, codes,
    mix_h, mix_v, bias_out, we, sn, w_in, b_in, w_mid, b_mid, w_out, sems
):
    fetch(
        [
            (mix_h_in, mix_h), (mix_v_in, mix_v), (bias_out_in, bias_out), (we_in, we),
            (sn_in, sn), (w_in_in, w_in), (b_in_in, b_in), (w_mid_in, w_mid), (b_mid_in, b_mid),
            (w_out_in, w_out),
        ],
        sems,
    )
    hidden = w_mid.shape[0]
    feature = w_in.shape[0]
    high = b_in[...].astype(BF).astype(F32)
    low = b_in[...] - high
    row = iota((32, hidden), 0)
    halves = []
    for l in range(2):
        r = iota((32, feature), 0)
        c = iota((32, feature), 1)
        chosen = (r < 24) & (((r >> 2) & 1) == l) & ((r >> 3) * 4 + (r & 3) == c)
        part = dot(jnp.where(chosen, 1.0, 0.0).astype(BF), w_in[...])
        part = jnp.where(row == 24, high, jnp.where(row == 25, low, part))
        halves.append(part)
    both = jnp.concatenate(halves, axis=1)
    in_back[...] = both.astype(BF)
    padded = jnp.concatenate([both, jnp.zeros((96, 2 * hidden), F32)], axis=0)
    in_all[...] = padded.T[:, :32].astype(BF)
    middle = w_mid[...].astype(F32)
    turned = middle.T
    zero = jnp.zeros((hidden, hidden), F32)
    for source, target in ((middle, mid_all), (turned, mid_back)):
        target[...] = jnp.concatenate(
            [jnp.concatenate([source, zero], axis=1), jnp.concatenate([zero, source], axis=1)],
            axis=0,
        ).astype(BF)
    column = jnp.broadcast_to(b_mid[...], (hidden, hidden)).T
    bias_mid[...] = jnp.concatenate([column, column], axis=0)
    out = w_out[...].astype(F32)
    empty = jnp.zeros((4, hidden), F32)
    upper = jnp.concatenate([out, empty], axis=0)
    lower = jnp.concatenate([empty, out], axis=0)
    wide_out = jnp.concatenate(
        [jnp.concatenate([upper, lower], axis=1), jnp.zeros((120, 2 * hidden), F32)], axis=0
    )
    out_all[...] = wide_out[:16].astype(BF)
    out_back[...] = wide_out.T[:, :16].astype(BF)
    r8 = iota((8, LANES), 0)
    f8 = r8 & 3

    def by_field(scalars):
        return jnp.where(
            f8 == 0,
            scalars[0],
            jnp.where(f8 == 1, scalars[1], jnp.where(f8 == 2, scalars[2], scalars[3])),
        )

    rows[0] = by_field(mix_h)
    rows[1] = jnp.where(r8 < 4, mix_v[0], mix_v[1])
    rows[2] = by_field(bias_out)
    here = lax.axis_index("tiles")
    half = lax.axis_index("sub")
    slots = codes.shape[1]
    for s in range(slots):
        for side in range(2):
            tile = we[side, s]
            safe = jnp.maximum(tile, 0)
            owner = jnp.bitwise_xor(lax.div(safe, slots), here)
            code = jnp.where(tile >= 0, owner * slots + lax.rem(safe, slots), -1)
            codes[side, s] = jnp.full((8, LANES), code, jnp.int32)
            code = jnp.where(half == side, sn[side, s], s)
            codes[2 + side, s] = jnp.full((8, LANES), code, jnp.int32)


def stencil(x, halos, cells):
    east, west, north, south = neighbours(x, halos, cells)
    diffuse = (east + west) + (north + south) - 4.0 * x
    ones = jnp.where(iota(x.shape, 0) < 2, 1.0, 0.0)
    features = jnp.concatenate([x, east - west, north - south, ones], axis=0).astype(BF)
    return diffuse, features


def keep_first(first_out, span, first):
    hidden = first.shape[0] // 2
    ones = jnp.ones((16, first.shape[1]), BF)
    for l in range(2):
        base = l * (hidden + 16)
        first_out[base : base + hidden, span] = first[l * hidden : (l + 1) * hidden]
        first_out[base + hidden : base + hidden + 16, span] = ones


def forward_kernel(
    peers, x_in, mask, above, below, partner, codes, in_all, mid_all, bias_mid, out_all, rows,
    *rest
):
    pools = rest[:peers]
    x_out, first_out, second_out, feature_out, columns, lines, closure = rest[peers:]
    slots = partner.shape[0]
    x = x_in[...]
    total = x.shape[1]
    cells = total // slots
    halos = halo_fields(codes, pools, partner, slots, cells)
    diffuse, features = stencil(x, halos, cells)
    feature_out[...] = features
    bias = wide(bias_mid[...], CHUNK // LANES)
    for start in range(0, total, CHUNK):
        span = slice(start, start + CHUNK)
        first = jnp.tanh(dot(in_all[...], feature_out[:, span])).astype(BF)
        keep_first(first_out, span, first)
        second = jnp.tanh(dot(mid_all[...], first) + bias).astype(BF)
        second_out[:, span] = second
        closure[:, span] = dot(out_all[...], second)[:8]
    mh, mv, bo = (wide(rows[k], total // LANES) for k in range(3))
    vertical = pltpu.roll(x, 4, 0) + level_halo(above, below, 0)
    x_new = mask[...] * (x + mh * diffuse + mv * (vertical - 2.0 * x) + (closure[...] + bo))
    x_out[...] = x_new
    write_edges(columns, lines, x_new, x_new, x_new, x_new)


def backward_tail(g, grad_feature, remote, rows, base, columns, lines, g_sum):
    total = g.shape[1]
    many = total // LANES
    cells = total // lines.shape[0]
    mh = wide(rows[0], many)
    mv = wide(rows[1], many)
    along = mh * g
    e_east = along + grad_feature[8:16]
    e_west = along - grad_feature[8:16]
    e_north = along + grad_feature[16:24]
    e_south = along - grad_feature[16:24]
    spread = mv * g
    vertical = pltpu.roll(spread, 4, 0) - 2.0 * spread
    if remote is not None:
        vertical = vertical + remote
    write_edges(columns, lines, e_west, e_east, e_south, e_north)
    base[...] = (
        (g + grad_feature[0:8])
        + (pull_back(e_east, e_west, e_north, e_south, cells) - 4.0 * along)
        + vertical
    )
    sums = [g[:, v * LANES : (v + 1) * LANES] for v in range(many)]
    g_sum[...] = tree_sum(sums)
    return spread


def grad_rows(g):
    return jnp.concatenate([g, jnp.zeros(g.shape, F32)], axis=0).astype(BF)


def seed_kernel(g_in, out_back, grad_out, seed_out):
    grad_out[...] = grad_rows(g_in[...])
    total = g_in.shape[1]
    for start in range(0, total, CHUNK):
        span = slice(start, start + CHUNK)
        seed_out[:, span] = dot(out_back[...], grad_out[:, span]).astype(BF)


def turn_kernel(
    peers, x_in, mask, g_in, seed, above, below, partner, codes, in_all, mid_all, bias_mid,
    out_all, rows, mid_back, in_back, *rest
):
    pools = rest[:peers]
    (
        x_out, base, columns, lines, g_sum, first_out, second_out, feature_out,
        second_grad_out, first_grad_out, closure, grad_feature,
    ) = rest[peers:]
    slots = partner.shape[0]
    x = x_in[...]
    g = g_in[...]
    total = x.shape[1]
    cells = total // slots
    halos = halo_fields(codes, pools, partner, slots, cells)
    diffuse, features = stencil(x, halos, cells)
    feature_out[...] = features
    bias = wide(bias_mid[...], CHUNK // LANES)
    for start in range(0, total, CHUNK):
        span = slice(start, start + CHUNK)
        first = jnp.tanh(dot(in_all[...], feature_out[:, span])).astype(BF)
        keep_first(first_out, span, first)
        second = jnp.tanh(dot(mid_all[...], first) + bias).astype(BF)
        second_out[:, span] = second
        closure[:, span] = dot(out_all[...], second)[:8]
        second_grad = times_slope(seed[:, span], second)
        second_grad_out[:, span] = second_grad
        first_grad = times_slope(dot(mid_back[...], second_grad), first)
        first_grad_out[:, span] = first_grad
        grad_feature[:, span] = dot(in_back[...], first_grad)
    remote = level_halo(above, below, 1)
    backward_tail(g, grad_feature[...], remote, rows, base, columns, lines, g_sum)
    mh, mv, bo = (wide(rows[k], total // LANES) for k in range(3))
    x_out[...] = mask[...] * (
        x + mh * diffuse + mv * (pltpu.roll(x, 4, 0) - 2.0 * x) + (closure[...] + bo)
    )


def times_slope(grad, value):
    return grad.astype(BF) * (1.0 - value * value)


def back_kernel(
    peers, base_in, mask, x_in, partner, codes, first_in, second_in, rows, out_back, mid_back,
    in_back, *rest
):
    pools = rest[:peers]
    base, columns, lines, g_sum, grad_out, second_grad_out, first_grad_out = rest[
        peers : peers + 7
    ]
    sends = rest[peers + 7 : -1]
    grad_feature = rest[-1]
    slots = partner.shape[0]
    total = base_in.shape[1]
    cells = total // slots
    hidden = mid_back.shape[0] // 2
    halos = halo_fields(codes, pools, partner, slots, cells)
    g = mask[...] * (base_in[...] + halo_sum(halos, cells))
    grad_out[...] = grad_rows(g)
    for start in range(0, total, CHUNK):
        span = slice(start, start + CHUNK)
        first = jnp.concatenate(
            [first_in[:hidden, span], first_in[hidden + 16 : 2 * hidden + 16, span]], axis=0
        )
        second_grad = times_slope(dot(out_back[...], grad_out[:, span]), second_in[:, span])
        second_grad_out[:, span] = second_grad
        first_grad = times_slope(dot(mid_back[...], second_grad), first)
        first_grad_out[:, span] = first_grad
        grad_feature[:, span] = dot(in_back[...], first_grad)
    spread = backward_tail(g, grad_feature[...], None, rows, base, columns, lines, g_sum)
    write_sends(sends, 0, x_in[...], cells)
    write_sends(sends, 1, spread, cells)


def term_sums(first, second, features, grad, second_grad, first_grad):
    hidden = first.shape[0] // 2 - 16
    side = hidden + 16
    mid = dot_nt(second_grad[:hidden], first[:side]) + dot_nt(second_grad[hidden:], first[side:])
    return mid, dot_nt(first_grad[...], features[...]), dot_nt(second[...], grad[...])


def late_terms_kernel(*refs):
    for value, out in zip(term_sums(*refs[:6]), refs[6:]):
        out[...] = value


def early_terms_kernel(*refs):
    late = refs[6:10]
    g_sum, keep, send = refs[10:]
    mid, wing, out = (a + b[...] for a, b in zip(term_sums(*refs[:6]), late[:3]))
    total = late[3][...] + g_sum[...]
    hidden = mid.shape[0]
    top = iota((8, hidden), 0)

    def turned(block):
        blank = jnp.zeros((block.shape[0], hidden - block.shape[1]), F32)
        return jnp.concatenate([block, blank], axis=1).T

    low, high = turned(wing[:hidden]), turned(wing[hidden:])
    kinds = [low[8 * k : 8 * k + 8] + pltpu.roll(high[8 * k : 8 * k + 8], 4, 0) for k in range(3)]
    bias_in = low[24:32] + high[24:32]
    bias_mid = turned(mid[:, hidden:])[:8]
    biases = jnp.where(top == 4, pltpu.roll(bias_in, 4, 0), pltpu.roll(bias_mid, 5, 0))
    low, high = turned(out[:hidden]), turned(out[hidden:])
    pieces = [
        mid[:, :hidden],
        jnp.where(top < 4, kinds[0], pltpu.roll(kinds[1], 4, 0)),
        jnp.where(top < 4, kinds[2], biases),
        jnp.where(top < 4, low[:8] + pltpu.roll(high[:8], 4, 0), total + pltpu.roll(total, 4, 0)),
        jnp.zeros((8, hidden), F32),
    ]
    packed = jnp.concatenate(pieces, axis=0)
    half = packed.shape[0] // 2
    core = lax.axis_index("sub")
    keep[...] = jnp.where(core == 0, packed[:half], packed[half:])
    send[...] = jnp.where(core == 0, packed[half:], packed[:half])


def finish_kernel(skip, base_in, mask, x_in, above, below, partner, codes, rows, *rest):
    pools = rest[:-3]
    final, initial, token = rest[-3:]
    token[...] = jnp.zeros(token.shape, F32)
    slots = partner.shape[0]
    total = base_in.shape[1]
    cells = total // slots
    mv = wide(rows[1], total // LANES)
    halos = halo_fields(codes, pools, partner, slots, cells, skip)
    last = x_in[...] + mask[...] * (mv * level_halo(above, below, 0))
    early = mask[...] * ((base_in[...] + level_halo(above, below, 1)) + halo_sum(halos, cells))
    for s in range(slots):
        span = slice(s * cells, (s + 1) * cells)
        for l in range(2):
            for f in range(4):
                r = 4 * l + f
                final[f, l, s : s + 1, :] = last[r : r + 1, span]
                initial[f, l, s : s + 1, :] = early[r : r + 1, span]


def grads_kernel(scale, mine, other, token, w_in, b_in, w_mid, b_mid, w_out, b_out):
    hidden = w_mid.shape[0]
    core = lax.axis_index("sub")
    low = jnp.where(core == 0, mine[...], other[...])
    high = jnp.where(core == 0, other[...], mine[...])
    packed = jnp.concatenate([low, high], axis=0) * scale
    w_mid[...] = packed[:hidden]
    tail = packed[hidden:]
    w_in[...] = tail[0:12]
    b_in[...] = tail[12:13]
    b_mid[...] = tail[13:14]
    w_out[...] = tail[16:20]
    for f in range(4):
        b_out[f] = jnp.sum(tail[20 + f : 21 + f])


def call(kernel, inputs, outs, scratch=(), spaces=None, scalars=0):
    if spaces is not None:
        inputs = [pltpu.with_memory_space_constraint(array, spaces) for array in inputs]
    return pl.pallas_call(
        kernel,
        in_specs=[pl.BlockSpec(memory_space=spaces or pltpu.VMEM)] * len(inputs),
        out_specs=[pl.BlockSpec(memory_space=pltpu.VMEM)] * (len(outs) - scalars)
        + [pl.BlockSpec(memory_space=pltpu.SMEM)] * scalars,
        out_shape=outs,
        scratch_shapes=list(scratch),
        compiler_params=pltpu.CompilerParams(vmem_limit_bytes=VMEM_BYTES),
    )(*inputs)


def shape(dims, dtype=F32):
    return jax.ShapeDtypeStruct(tuple(dims), dtype)


def xor_pairs(axis, k):
    return [(i, i ^ k) for i in range(lax.axis_size(axis))]


def from_peers(packs):
    return [packs] + [
        lax.ppermute(packs, "tiles", xor_pairs("tiles", k))
        for k in range(1, lax.axis_size("tiles"))
    ]


def from_partner(lines):
    return lax.ppermute(lines, "sub", xor_pairs("sub", 1))


def from_levels(sends):
    depth = lax.axis_size("depth")
    if len(sends) == 1:
        other = lax.ppermute(sends[0], "depth", [(0, 1), (1, 0)])
        return other, other
    down = [(i, i + 1) for i in range(depth - 1)]
    return (
        lax.ppermute(sends[0], "depth", down),
        lax.ppermute(sends[1], "depth", [(j, i) for i, j in down]),
    )


def tree_sum(parts):
    while len(parts) > 1:
        parts = [parts[i] + parts[i + 1] for i in range(0, len(parts), 2)]
    return parts[0]


def sum_over(array, axis):
    return tree_sum(
        [array]
        + [lax.ppermute(array, axis, xor_pairs(axis, k)) for k in range(1, lax.axis_size(axis))]
    )


def body(
    state_init,
    cotangent,
    level_count,
    west_east,
    south_north,
    weight_in,
    bias_in,
    weight_mid,
    bias_mid,
    weight_out,
    bias_out,
    mix_horizontal,
    mix_vertical,
):
    _, levels, slots, cells = state_init.shape
    hidden = weight_mid.shape[0]
    both = 2 * hidden
    total = slots * cells
    peers = lax.axis_size("tiles")
    field = shape((8, total))
    column_pack = shape((slots // 2, 8, LANES))
    line_pack = shape((slots, 8, LANES))
    sends = [shape((2, slots // 2, 8, cells))] * (1 if lax.axis_size("depth") == 2 else 2)
    hidden_rows = shape((both, total), BF)
    first_rows = shape((both + 32, total), BF)
    vmem, smem = pltpu.VMEM, pltpu.SMEM

    inputs = [mix_vertical, state_init, cotangent, level_count]
    x_zero, g_late, mask, columns, lines, *levels_out = call(
        functools.partial(prep_kernel, len(sends)),
        inputs,
        [field, field, field, column_pack, line_pack] + sends,
        [
            smem(mix_vertical.shape, F32),
            vmem(state_init.shape, F32),
            vmem(cotangent.shape, F32),
            vmem(level_count.shape, jnp.int32),
            pltpu.SemaphoreType.DMA((len(inputs),)),
        ],
        pltpu.HBM,
    )
    above, below = from_levels(levels_out)
    pools = from_peers(columns)
    partner = from_partner(lines)

    inputs = [
        mix_horizontal,
        mix_vertical,
        bias_out,
        west_east.T,
        south_north.T,
        weight_in.T,
        bias_in.reshape(1, hidden),
        weight_mid,
        bias_mid.reshape(1, hidden),
        weight_out,
    ]
    in_all, in_back, mid_all, mid_back, mid_bias, out_all, out_back, rows, codes = call(
        weight_kernel,
        inputs,
        [
            shape((both, 32), BF),
            shape((32, both), BF),
            shape((both, both), BF),
            shape((both, both), BF),
            shape((both, hidden)),
            shape((16, both), BF),
            shape((both, 16), BF),
            shape((3, 8, LANES)),
            shape((4, slots, 8, LANES), jnp.int32),
        ],
        [(smem if i < 5 else vmem)(a.shape, a.dtype) for i, a in enumerate(inputs)]
        + [pltpu.SemaphoreType.DMA((len(inputs),))],
        pltpu.HBM,
    )
    forward_weights = [in_all, mid_all, mid_bias, out_all, rows]
    backward_weights = [out_back, mid_back, in_back]

    late_grad, seed = call(seed_kernel, [g_late, out_back], [shape((16, total), BF), hidden_rows])

    x_one, first, second, features, columns, lines = call(
        functools.partial(forward_kernel, peers),
        [x_zero, mask, above, below, partner, codes] + forward_weights + pools,
        [field, first_rows, hidden_rows, shape((32, total), BF), column_pack, line_pack],
        [vmem((8, total), F32)],
    )
    pools = from_peers(columns)
    partner = from_partner(lines)

    x_two, base, columns, lines, late_sum, *late = call(
        functools.partial(turn_kernel, peers),
        [x_one, mask, g_late, seed, above, below, partner, codes]
        + forward_weights
        + backward_weights[1:]
        + pools,
        [
            field, field, column_pack, line_pack, shape((8, LANES)), first_rows, hidden_rows,
            shape((32, total), BF), hidden_rows, hidden_rows,
        ],
        [vmem((8, total), F32), vmem((32, total), F32)],
    )
    pools = from_peers(columns)
    partner = from_partner(lines)
    late = call(
        late_terms_kernel,
        late[:3] + [late_grad] + late[3:],
        [shape((hidden, hidden + 16)), shape((both, 32)), shape((both, 16))],
    )

    late, base = lax.optimization_barrier((late, base))
    base, columns, lines, early_sum, grad, second_grad, first_grad, *levels_out = call(
        functools.partial(back_kernel, peers),
        [base, mask, x_one, partner, codes, first, second, rows] + backward_weights + pools,
        [
            field, column_pack, line_pack, shape((8, LANES)), shape((16, total), BF), hidden_rows, hidden_rows,
        ]
        + sends,
        [vmem((32, total), F32)],
    )
    above, below = from_levels(levels_out)
    partner = from_partner(lines)
    half = shape(((hidden + 32) // 2, hidden))
    keep, give = call(
        early_terms_kernel,
        [first, second, features, grad, second_grad, first_grad, *late, late_sum, early_sum],
        [half, half],
    )
    terms = keep + lax.ppermute(give, "sub", xor_pairs("sub", 1))
    terms, above, below, partner = lax.optimization_barrier((terms, above, below, partner))
    parts = from_peers(jnp.concatenate([terms, columns.reshape(slots * 4, LANES)], axis=0))
    terms = tree_sum([part[: half.shape[0]] for part in parts])
    terms = sum_over(terms, "depth")
    final_state, initial_cot, token = call(
        functools.partial(finish_kernel, half.shape[0]),
        [base, mask, x_two, above, below, partner, codes, rows] + parts,
        [shape(state_init.shape)] * 2 + [shape((8, LANES))],
    )
    terms, token = lax.optimization_barrier((terms, token))
    count = (
        levels
        * lax.axis_size("depth")
        * slots
        * lax.axis_size("tiles")
        * cells
        * lax.axis_size("sub")
    )
    w_in, b_in, w_mid, b_mid, w_out, b_out = call(
        functools.partial(grads_kernel, 1.0 / math.sqrt(count)),
        [terms, lax.ppermute(terms, "sub", xor_pairs("sub", 1)), token],
        [
            shape(weight_in.T.shape),
            shape((1, hidden)),
            shape((hidden, hidden)),
            shape((1, hidden)),
            shape(weight_out.shape),
            shape(bias_out.shape),
        ],
        scalars=1,
    )
    return (
        final_state,
        initial_cot,
        w_in.T,
        b_in.reshape(hidden),
        w_mid,
        b_mid.reshape(hidden),
        w_out,
        b_out,
    )


def solution(mesh):
    return jax.shard_map(
        body,
        mesh=mesh,
        in_specs=(
            P("groups", "depth", "tiles", "sub"),
            P("groups", "depth", "tiles", "sub"),
            P("tiles", "sub"),
            P("tiles", None),
            P("tiles", None),
            P(),
            P(),
            P(),
            P(),
            P(),
            P(),
            P(),
            P("depth"),
        ),
        out_specs=(
            P("groups", "depth", "tiles", "sub"),
            P("groups", "depth", "tiles", "sub"),
            P("groups", None),
            P("groups"),
            P("groups", None),
            P("groups"),
            P("groups", None),
            P("groups"),
        ),
        check_vma=False,
    )
```

```python
import functools
import math

import jax
import jax.numpy as jnp
from jax import lax
from jax.experimental import pallas as pl
from jax.experimental.pallas import tpu as pltpu
from jax.sharding import PartitionSpec as P

TCOL = 64
LANES = 128
CHUNK = 2048
BF = jnp.bfloat16
F32 = jnp.float32
VMEM_BYTES = 16 * 1024 * 1024
NT = (((1,), (1,)), ((), ()))


def dot(left, right):
    return jnp.dot(left, right, preferred_element_type=F32)


def dot_nt(left, right):
    return lax.dot_general(left, right, NT, preferred_element_type=F32)


def iota(shape, axis):
    return lax.broadcasted_iota(jnp.int32, shape, axis)


def wide(block, copies):
    return jnp.concatenate([block] * copies, axis=1)


def pack_columns(first, last, place_of_slot):
    place = iota((8, LANES), 1) & 63
    packed = jnp.zeros((8, LANES), F32)
    for v in range(first.shape[1] // LANES):
        span = slice(v * LANES, (v + 1) * LANES)
        at = v + place_of_slot
        low = pltpu.roll(first[:, span], at, 1) if at else first[:, span]
        high = pltpu.roll(last[:, span], at + 17, 1)
        packed = jnp.where(place == at, low, packed)
        packed = jnp.where(place == at + 16, high, packed)
    return packed


def pack_lines(first, last):
    cells = first.shape[1]
    lane = iota((8, LANES), 1)
    return jnp.where(lane < TCOL, first[:, :LANES], last[:, cells - LANES :])


def halo_fields(codes, pools, partner, slots, cells, skip=None):
    lane = iota((8, LANES), 1)
    count = cells // LANES
    east, west, lines = [], [], []

    def chosen(code, blocks):
        found = jnp.zeros((8, LANES), F32)
        for k, block in enumerate(blocks):
            found = jnp.where(code == k, block, found)
        return found

    column_blocks = []
    for pool in pools:
        for i in range(slots // 2):
            both = pool[i] if skip is None else pool[skip + 8 * i : skip + 8 * i + 8]
            column_blocks += [both, pltpu.roll(both, LANES - 32, 1)]
    line_blocks = [partner[s] for s in range(slots)]
    for s in range(slots):
        west_pack = chosen(codes[0, s], column_blocks)
        east_pack = chosen(codes[1, s], column_blocks)
        south = pltpu.roll(chosen(codes[2, s], line_blocks), TCOL, 1)
        north = pltpu.roll(chosen(codes[3, s], line_blocks), TCOL, 1)
        east += [pltpu.roll(east_pack, 63 - v, 1) for v in range(count)]
        west += [pltpu.roll(west_pack, 48 - v, 1) for v in range(count)]
        lines += [jnp.where(lane < TCOL, south, north)] * count
    return tuple(jnp.concatenate(part, axis=1) for part in (east, west, lines))


def places(shape, cells):
    lane = iota(shape, 1) & (cells - 1)
    column = lane & (TCOL - 1)
    return column == TCOL - 1, column == 0, lane >= cells - TCOL, lane < TCOL


def neighbours(x, halos, cells):
    total = x.shape[1]
    east_halo, west_halo, lines = halos
    at_east, at_west, at_north, at_south = places(x.shape, cells)
    east = jnp.where(at_east, east_halo, pltpu.roll(x, total - 1, 1))
    west = jnp.where(at_west, west_halo, pltpu.roll(x, 1, 1))
    north = jnp.where(at_north, lines, pltpu.roll(x, total - TCOL, 1))
    south = jnp.where(at_south, lines, pltpu.roll(x, TCOL, 1))
    return east, west, north, south


def halo_sum(halos, cells):
    east_halo, west_halo, lines = halos
    at_east, at_west, at_north, at_south = places(lines.shape, cells)
    columns = jnp.where(at_east, east_halo, jnp.where(at_west, west_halo, 0.0))
    return columns + jnp.where(at_north | at_south, lines, 0.0)


def pull_back(e_east, e_west, e_north, e_south, cells):
    total = e_east.shape[1]
    at_east, at_west, at_north, at_south = places(e_east.shape, cells)
    return (
        jnp.where(at_west, 0.0, pltpu.roll(e_east, 1, 1))
        + jnp.where(at_east, 0.0, pltpu.roll(e_west, total - 1, 1))
    ) + (
        jnp.where(at_south, 0.0, pltpu.roll(e_north, TCOL, 1))
        + jnp.where(at_north, 0.0, pltpu.roll(e_south, total - TCOL, 1))
    )


def write_edges(columns, lines, first_column, last_column, first_line, last_line):
    slots = lines.shape[0]
    cells = first_column.shape[1] // slots
    spans = [slice(s * cells, (s + 1) * cells) for s in range(slots)]
    packs = [
        pack_columns(first_column[:, span], last_column[:, span], 32 * (s % 2))
        for s, span in enumerate(spans)
    ]
    for s, span in enumerate(spans):
        if s % 2 == 0:
            columns[s // 2] = packs[s] + packs[s + 1]
        lines[s] = pack_lines(first_line[:, span], last_line[:, span])


def write_sends(sends, kind, x, cells):
    depth = lax.axis_index("depth")
    top = iota((8, cells), 0) < 4
    for i in range(x.shape[1] // (2 * cells)):
        even = x[:, 2 * i * cells : (2 * i + 1) * cells]
        odd = x[:, (2 * i + 1) * cells : (2 * i + 2) * cells]
        down = jnp.where(top, pltpu.roll(even, 4, 0), odd)
        up = jnp.where(top, even, pltpu.roll(odd, 4, 0))
        if len(sends) == 1:
            sends[0][kind, i] = jnp.where(depth == 0, down, up)
        else:
            sends[0][kind, i] = down
            sends[1][kind, i] = up


def level_halo(above_ref, below_ref, kind):
    depth = lax.axis_index("depth")
    last = lax.axis_size("depth") - 1
    parts = []
    for i in range(above_ref.shape[1]):
        above = jnp.where(depth > 0, above_ref[kind, i], 0.0)
        below = jnp.where(depth < last, below_ref[kind, i], 0.0)
        top = iota(above.shape, 0) < 4
        parts.append(jnp.where(top, above, pltpu.roll(below, 4, 0)))
        parts.append(jnp.where(top, pltpu.roll(above, 4, 0), below))
    return jnp.concatenate(parts, axis=1)


def fetch(pairs, sems):
    copies = [
        pltpu.make_async_copy(source, target, sems.at[i])
        for i, (source, target) in enumerate(pairs)
    ]
    for copy in copies:
        copy.start()
    for copy in copies:
        copy.wait()


def prep_kernel(sent, mix_v_in, state_in, cot_in, count_in, *rest):
    x_out, g_out, mask_out, columns, lines = rest[:5]
    sends = rest[5 : 5 + sent]
    mix_v, state, cot, count, sems = rest[5 + sent :]
    fetch(
        [(mix_v_in, mix_v), (count_in, count), (state_in, state), (cot_in, cot)], sems
    )
    slots = state.shape[2]
    cells = state.shape[3]
    depth = lax.axis_index("depth")
    for s in range(slots):
        span = slice(s * cells, (s + 1) * cells)
        for l in range(2):
            for f in range(4):
                r = 4 * l + f
                x_out[r : r + 1, span] = state[f, l, s : s + 1, :]
                g_out[r : r + 1, span] = cot[f, l, s : s + 1, :]
    deep = jnp.concatenate(
        [jnp.broadcast_to(count[s : s + 1, :], (8, cells)) for s in range(slots)], axis=1
    )
    upper = iota(deep.shape, 0) < 4
    mask = jnp.where(2 * depth + jnp.where(upper, 0, 1) < deep, 1.0, 0.0)
    x = mask * x_out[...]
    g = mask * g_out[...]
    mask_out[...] = mask
    x_out[...] = x
    g_out[...] = g
    write_edges(columns, lines, x, x, x, x)
    write_sends(sends, 0, x, cells)
    write_sends(sends, 1, jnp.where(upper, mix_v[0], mix_v[1]) * g, cells)


def weight_kernel(
    mix_h_in, mix_v_in, bias_out_in, we_in, sn_in, w_in_in, b_in_in, w_mid_in, b_mid_in, w_out_in,
    in_all, in_back, mid_all, mid_back, bias_mid, out_all, out_back, rows, codes,
    mix_h, mix_v, bias_out, we, sn, w_in, b_in, w_mid, b_mid, w_out, sems
):
    fetch(
        [
            (mix_h_in, mix_h), (mix_v_in, mix_v), (bias_out_in, bias_out), (we_in, we),
            (sn_in, sn), (w_in_in, w_in), (b_in_in, b_in), (w_mid_in, w_mid), (b_mid_in, b_mid),
            (w_out_in, w_out),
        ],
        sems,
    )
    hidden = w_mid.shape[0]
    feature = w_in.shape[0]
    high = b_in[...].astype(BF).astype(F32)
    low = b_in[...] - high
    row = iota((32, hidden), 0)
    halves = []
    for l in range(2):
        r = iota((32, feature), 0)
        c = iota((32, feature), 1)
        chosen = (r < 24) & (((r >> 2) & 1) == l) & ((r >> 3) * 4 + (r & 3) == c)
        part = dot(jnp.where(chosen, 1.0, 0.0).astype(BF), w_in[...])
        part = jnp.where(row == 24, high, jnp.where(row == 25, low, part))
        halves.append(part)
    both = jnp.concatenate(halves, axis=1)
    in_back[...] = both.astype(BF)
    padded = jnp.concatenate([both, jnp.zeros((96, 2 * hidden), F32)], axis=0)
    in_all[...] = padded.T[:, :32].astype(BF)
    middle = w_mid[...].astype(F32)
    turned = middle.T
    zero = jnp.zeros((hidden, hidden), F32)
    for source, target in ((middle, mid_all), (turned, mid_back)):
        target[...] = jnp.concatenate(
            [jnp.concatenate([source, zero], axis=1), jnp.concatenate([zero, source], axis=1)],
            axis=0,
        ).astype(BF)
    column = jnp.broadcast_to(b_mid[...], (hidden, hidden)).T
    bias_mid[...] = jnp.concatenate([column, column], axis=0)
    out = w_out[...].astype(F32)
    empty = jnp.zeros((4, hidden), F32)
    upper = jnp.concatenate([out, empty], axis=0)
    lower = jnp.concatenate([empty, out], axis=0)
    wide_out = jnp.concatenate(
        [jnp.concatenate([upper, lower], axis=1), jnp.zeros((120, 2 * hidden), F32)], axis=0
    )
    out_all[...] = wide_out[:16].astype(BF)
    out_back[...] = wide_out.T[:, :16].astype(BF)
    r8 = iota((8, LANES), 0)
    f8 = r8 & 3

    def by_field(scalars):
        return jnp.where(
            f8 == 0,
            scalars[0],
            jnp.where(f8 == 1, scalars[1], jnp.where(f8 == 2, scalars[2], scalars[3])),
        )

    rows[0] = by_field(mix_h)
    rows[1] = jnp.where(r8 < 4, mix_v[0], mix_v[1])
    rows[2] = by_field(bias_out)
    here = lax.axis_index("tiles")
    half = lax.axis_index("sub")
    slots = codes.shape[1]
    for s in range(slots):
        for side in range(2):
            tile = we[side, s]
            safe = jnp.maximum(tile, 0)
            owner = jnp.bitwise_xor(lax.div(safe, slots), here)
            code = jnp.where(tile >= 0, owner * slots + lax.rem(safe, slots), -1)
            codes[side, s] = jnp.full((8, LANES), code, jnp.int32)
            code = jnp.where(half == side, sn[side, s], s)
            codes[2 + side, s] = jnp.full((8, LANES), code, jnp.int32)


def stencil(x, halos, cells):
    east, west, north, south = neighbours(x, halos, cells)
    diffuse = (east + west) + (north + south) - 4.0 * x
    ones = jnp.where(iota(x.shape, 0) < 2, 1.0, 0.0)
    features = jnp.concatenate([x, east - west, north - south, ones], axis=0).astype(BF)
    return diffuse, features


def keep_first(first_out, span, first):
    hidden = first.shape[0] // 2
    ones = jnp.ones((16, first.shape[1]), BF)
    for l in range(2):
        base = l * (hidden + 16)
        first_out[base : base + hidden, span] = first[l * hidden : (l + 1) * hidden]
        first_out[base + hidden : base + hidden + 16, span] = ones


def forward_kernel(
    peers, x_in, mask, above, below, partner, codes, in_all, mid_all, bias_mid, out_all, rows,
    *rest
):
    pools = rest[:peers]
    x_out, first_out, second_out, feature_out, columns, lines, closure = rest[peers:]
    slots = partner.shape[0]
    x = x_in[...]
    total = x.shape[1]
    cells = total // slots
    halos = halo_fields(codes, pools, partner, slots, cells)
    diffuse, features = stencil(x, halos, cells)
    feature_out[...] = features
    bias = wide(bias_mid[...], CHUNK // LANES)
    for start in range(0, total, CHUNK):
        span = slice(start, start + CHUNK)
        first = jnp.tanh(dot(in_all[...], feature_out[:, span])).astype(BF)
        keep_first(first_out, span, first)
        second = jnp.tanh(dot(mid_all[...], first) + bias).astype(BF)
        second_out[:, span] = second
        closure[:, span] = dot(out_all[...], second)[:8]
    mh, mv, bo = (wide(rows[k], total // LANES) for k in range(3))
    vertical = pltpu.roll(x, 4, 0) + level_halo(above, below, 0)
    x_new = mask[...] * (x + mh * diffuse + mv * (vertical - 2.0 * x) + (closure[...] + bo))
    x_out[...] = x_new
    write_edges(columns, lines, x_new, x_new, x_new, x_new)


def backward_tail(g, grad_feature, remote, rows, base, columns, lines, g_sum):
    total = g.shape[1]
    many = total // LANES
    cells = total // lines.shape[0]
    mh = wide(rows[0], many)
    mv = wide(rows[1], many)
    along = mh * g
    e_east = along + grad_feature[8:16]
    e_west = along - grad_feature[8:16]
    e_north = along + grad_feature[16:24]
    e_south = along - grad_feature[16:24]
    spread = mv * g
    vertical = pltpu.roll(spread, 4, 0) - 2.0 * spread
    if remote is not None:
        vertical = vertical + remote
    write_edges(columns, lines, e_west, e_east, e_south, e_north)
    base[...] = (
        (g + grad_feature[0:8])
        + (pull_back(e_east, e_west, e_north, e_south, cells) - 4.0 * along)
        + vertical
    )
    sums = [g[:, v * LANES : (v + 1) * LANES] for v in range(many)]
    g_sum[...] = tree_sum(sums)


def grad_rows(g):
    return jnp.concatenate([g, jnp.zeros(g.shape, F32)], axis=0).astype(BF)


def seed_kernel(g_in, out_back, grad_out, seed_out):
    grad_out[...] = grad_rows(g_in[...])
    total = g_in.shape[1]
    for start in range(0, total, CHUNK):
        span = slice(start, start + CHUNK)
        seed_out[:, span] = dot(out_back[...], grad_out[:, span]).astype(BF)


def turn_kernel(
    peers, x_in, mask, g_in, seed, above, below, partner, codes, in_all, mid_all, bias_mid,
    out_all, rows, mid_back, in_back, *rest
):
    pools = rest[:peers]
    (
        x_out, base, columns, lines, g_sum, first_out, second_out, feature_out,
        second_grad_out, first_grad_out, closure, grad_feature,
    ) = rest[peers:]
    slots = partner.shape[0]
    x = x_in[...]
    g = g_in[...]
    total = x.shape[1]
    cells = total // slots
    halos = halo_fields(codes, pools, partner, slots, cells)
    diffuse, features = stencil(x, halos, cells)
    feature_out[...] = features
    bias = wide(bias_mid[...], CHUNK // LANES)
    for start in range(0, total, CHUNK):
        span = slice(start, start + CHUNK)
        first = jnp.tanh(dot(in_all[...], feature_out[:, span])).astype(BF)
        keep_first(first_out, span, first)
        second = jnp.tanh(dot(mid_all[...], first) + bias).astype(BF)
        second_out[:, span] = second
        closure[:, span] = dot(out_all[...], second)[:8]
        second_grad = times_slope(seed[:, span], second)
        second_grad_out[:, span] = second_grad
        first_grad = times_slope(dot(mid_back[...], second_grad), first)
        first_grad_out[:, span] = first_grad
        grad_feature[:, span] = dot(in_back[...], first_grad)
    remote = level_halo(above, below, 1)
    backward_tail(g, grad_feature[...], remote, rows, base, columns, lines, g_sum)
    mh, mv, bo = (wide(rows[k], total // LANES) for k in range(3))
    x_out[...] = mask[...] * (
        x + mh * diffuse + mv * (pltpu.roll(x, 4, 0) - 2.0 * x) + (closure[...] + bo)
    )


def times_slope(grad, value):
    return grad.astype(BF) * (1.0 - value * value)


def arrive_kernel(peers, base_in, mask, x_in, partner, codes, rows, *rest):
    pools = rest[:peers]
    g_out = rest[peers]
    sends = rest[peers + 1 :]
    slots = partner.shape[0]
    total = base_in.shape[1]
    cells = total // slots
    halos = halo_fields(codes, pools, partner, slots, cells)
    g = mask[...] * (base_in[...] + halo_sum(halos, cells))
    g_out[...] = g
    write_sends(sends, 0, x_in[...], cells)
    write_sends(sends, 1, wide(rows[1], total // LANES) * g, cells)


def back_kernel(
    g_in, first_in, second_in, rows, out_back, mid_back, in_back, base, columns, lines, g_sum,
    grad_out, second_grad_out, first_grad_out, grad_feature
):
    g = g_in[...]
    total = g.shape[1]
    hidden = mid_back.shape[0] // 2
    grad_out[...] = grad_rows(g)
    for start in range(0, total, CHUNK):
        span = slice(start, start + CHUNK)
        first = jnp.concatenate(
            [first_in[:hidden, span], first_in[hidden + 16 : 2 * hidden + 16, span]], axis=0
        )
        second_grad = times_slope(dot(out_back[...], grad_out[:, span]), second_in[:, span])
        second_grad_out[:, span] = second_grad
        first_grad = times_slope(dot(mid_back[...], second_grad), first)
        first_grad_out[:, span] = first_grad
        grad_feature[:, span] = dot(in_back[...], first_grad)
    backward_tail(g, grad_feature[...], None, rows, base, columns, lines, g_sum)


def middle_sums(first, second_grad):
    hidden = first.shape[0] // 2 - 16
    side = hidden + 16
    return dot_nt(second_grad[:hidden], first[:side]) + dot_nt(second_grad[hidden:], first[side:])


def outer_sums(second, features, grad, first_grad):
    return dot_nt(first_grad[...], features[...]), dot_nt(second[...], grad[...])


def late_terms_kernel(first, second, features, grad, second_grad, first_grad, mid, wing, out):
    mid[...] = middle_sums(first, second_grad)
    wing[...], out[...] = outer_sums(second, features, grad, first_grad)


def middle_kernel(first, second_grad, late, keep, send, bias):
    total = late[...] + middle_sums(first, second_grad)
    half, hidden = keep.shape
    core = lax.axis_index("sub")
    low, high = total[:half, :hidden], total[half:, :hidden]
    keep[...] = jnp.where(core == 0, low, high)
    send[...] = jnp.where(core == 0, high, low)
    bias[...] = total[:, hidden:]


def outer_kernel(
    second, features, grad, first_grad, late_wing, late_out, late_sum, early_sum, middle_bias,
    packed
):
    wing, out = outer_sums(second, features, grad, first_grad)
    wing = wing + late_wing[...]
    out = out + late_out[...]
    total = late_sum[...] + early_sum[...]
    hidden = wing.shape[0] // 2
    top = iota((8, hidden), 0)

    def turned(block):
        blank = jnp.zeros((block.shape[0], hidden - block.shape[1]), F32)
        return jnp.concatenate([block, blank], axis=1).T

    low, high = turned(wing[:hidden]), turned(wing[hidden:])
    kinds = [low[8 * k : 8 * k + 8] + pltpu.roll(high[8 * k : 8 * k + 8], 4, 0) for k in range(3)]
    bias_in = low[24:32] + high[24:32]
    bias_mid = turned(middle_bias[...])[:8]
    biases = jnp.where(top == 4, pltpu.roll(bias_in, 4, 0), pltpu.roll(bias_mid, 5, 0))
    low, high = turned(out[:hidden]), turned(out[hidden:])
    packed[0:8] = jnp.where(top < 4, kinds[0], pltpu.roll(kinds[1], 4, 0))
    packed[8:16] = jnp.where(top < 4, kinds[2], biases)
    packed[16:24] = jnp.where(
        top < 4, low[:8] + pltpu.roll(high[:8], 4, 0), total + pltpu.roll(total, 4, 0)
    )


def finish_kernel(skip, base_in, mask, x_in, above, below, partner, codes, rows, *rest):
    pools = rest[:-3]
    final, initial, token = rest[-3:]
    token[...] = jnp.zeros(token.shape, F32)
    slots = partner.shape[0]
    total = base_in.shape[1]
    cells = total // slots
    mv = wide(rows[1], total // LANES)
    halos = halo_fields(codes, pools, partner, slots, cells, skip)
    last = x_in[...] + mask[...] * (mv * level_halo(above, below, 0))
    early = mask[...] * ((base_in[...] + level_halo(above, below, 1)) + halo_sum(halos, cells))
    for s in range(slots):
        span = slice(s * cells, (s + 1) * cells)
        for l in range(2):
            for f in range(4):
                r = 4 * l + f
                final[f, l, s : s + 1, :] = last[r : r + 1, span]
                initial[f, l, s : s + 1, :] = early[r : r + 1, span]


def grads_kernel(scale, mine, other, token, w_in, b_in, w_mid, b_mid, w_out, b_out):
    hidden = w_mid.shape[0]
    core = lax.axis_index("sub")
    half = hidden // 2
    w_mid[:half] = jnp.where(core == 0, mine[:half], other[:half]) * scale
    w_mid[half:] = jnp.where(core == 0, other[:half], mine[:half]) * scale
    tail = (mine[half:] + other[half:]) * scale
    w_in[...] = tail[0:12]
    b_in[...] = tail[12:13]
    b_mid[...] = tail[13:14]
    w_out[...] = tail[16:20]
    for f in range(4):
        b_out[f] = jnp.sum(tail[20 + f : 21 + f])


def call(kernel, inputs, outs, scratch=(), spaces=None, scalars=0):
    if spaces is not None:
        inputs = [pltpu.with_memory_space_constraint(array, spaces) for array in inputs]
    return pl.pallas_call(
        kernel,
        in_specs=[pl.BlockSpec(memory_space=spaces or pltpu.VMEM)] * len(inputs),
        out_specs=[pl.BlockSpec(memory_space=pltpu.VMEM)] * (len(outs) - scalars)
        + [pl.BlockSpec(memory_space=pltpu.SMEM)] * scalars,
        out_shape=outs,
        scratch_shapes=list(scratch),
        compiler_params=pltpu.CompilerParams(vmem_limit_bytes=VMEM_BYTES),
    )(*inputs)


def shape(dims, dtype=F32):
    return jax.ShapeDtypeStruct(tuple(dims), dtype)


def xor_pairs(axis, k):
    return [(i, i ^ k) for i in range(lax.axis_size(axis))]


def from_peers(packs):
    return [packs] + [
        lax.ppermute(packs, "tiles", xor_pairs("tiles", k))
        for k in range(1, lax.axis_size("tiles"))
    ]


def from_partner(lines):
    return lax.ppermute(lines, "sub", xor_pairs("sub", 1))


def from_levels(sends):
    depth = lax.axis_size("depth")
    if len(sends) == 1:
        other = lax.ppermute(sends[0], "depth", [(0, 1), (1, 0)])
        return other, other
    down = [(i, i + 1) for i in range(depth - 1)]
    return (
        lax.ppermute(sends[0], "depth", down),
        lax.ppermute(sends[1], "depth", [(j, i) for i, j in down]),
    )


def tree_sum(parts):
    while len(parts) > 1:
        parts = [parts[i] + parts[i + 1] for i in range(0, len(parts), 2)]
    return parts[0]


def sum_over(array, axis):
    return tree_sum(
        [array]
        + [lax.ppermute(array, axis, xor_pairs(axis, k)) for k in range(1, lax.axis_size(axis))]
    )


def total_halves(terms):
    if lax.axis_size("depth") > 2:
        mine = sum_over(terms, "depth")
        return mine, lax.ppermute(mine, "sub", xor_pairs("sub", 1))
    crossed = lax.ppermute(terms, ("depth", "sub"), [(i, i ^ 3) for i in range(4)])
    below = lax.ppermute(terms, "depth", xor_pairs("depth", 1))
    beside = lax.ppermute(terms, "sub", xor_pairs("sub", 1))
    return terms + below, beside + crossed


def body(
    state_init,
    cotangent,
    level_count,
    west_east,
    south_north,
    weight_in,
    bias_in,
    weight_mid,
    bias_mid,
    weight_out,
    bias_out,
    mix_horizontal,
    mix_vertical,
):
    _, levels, slots, cells = state_init.shape
    hidden = weight_mid.shape[0]
    both = 2 * hidden
    total = slots * cells
    peers = lax.axis_size("tiles")
    field = shape((8, total))
    column_pack = shape((slots // 2, 8, LANES))
    line_pack = shape((slots, 8, LANES))
    sends = [shape((2, slots // 2, 8, cells))] * (1 if lax.axis_size("depth") == 2 else 2)
    hidden_rows = shape((both, total), BF)
    first_rows = shape((both + 32, total), BF)
    vmem, smem = pltpu.VMEM, pltpu.SMEM

    inputs = [mix_vertical, state_init, cotangent, level_count]
    x_zero, g_late, mask, columns, lines, *levels_out = call(
        functools.partial(prep_kernel, len(sends)),
        inputs,
        [field, field, field, column_pack, line_pack] + sends,
        [
            smem(mix_vertical.shape, F32),
            vmem(state_init.shape, F32),
            vmem(cotangent.shape, F32),
            vmem(level_count.shape, jnp.int32),
            pltpu.SemaphoreType.DMA((len(inputs),)),
        ],
        pltpu.HBM,
    )
    above, below = from_levels(levels_out)
    pools = from_peers(columns)
    partner = from_partner(lines)

    inputs = [
        mix_horizontal,
        mix_vertical,
        bias_out,
        west_east.T,
        south_north.T,
        weight_in.T,
        bias_in.reshape(1, hidden),
        weight_mid,
        bias_mid.reshape(1, hidden),
        weight_out,
    ]
    in_all, in_back, mid_all, mid_back, mid_bias, out_all, out_back, rows, codes = call(
        weight_kernel,
        inputs,
        [
            shape((both, 32), BF),
            shape((32, both), BF),
            shape((both, both), BF),
            shape((both, both), BF),
            shape((both, hidden)),
            shape((16, both), BF),
            shape((both, 16), BF),
            shape((3, 8, LANES)),
            shape((4, slots, 8, LANES), jnp.int32),
        ],
        [(smem if i < 5 else vmem)(a.shape, a.dtype) for i, a in enumerate(inputs)]
        + [pltpu.SemaphoreType.DMA((len(inputs),))],
        pltpu.HBM,
    )
    forward_weights = [in_all, mid_all, mid_bias, out_all, rows]
    backward_weights = [out_back, mid_back, in_back]

    late_grad, seed = call(seed_kernel, [g_late, out_back], [shape((16, total), BF), hidden_rows])

    x_one, first, second, features, columns, lines = call(
        functools.partial(forward_kernel, peers),
        [x_zero, mask, above, below, partner, codes] + forward_weights + pools,
        [field, first_rows, hidden_rows, shape((32, total), BF), column_pack, line_pack],
        [vmem((8, total), F32)],
    )
    pools = from_peers(columns)
    partner = from_partner(lines)

    x_two, base, columns, lines, late_sum, *late = call(
        functools.partial(turn_kernel, peers),
        [x_one, mask, g_late, seed, above, below, partner, codes]
        + forward_weights
        + backward_weights[1:]
        + pools,
        [
            field, field, column_pack, line_pack, shape((8, LANES)), first_rows, hidden_rows,
            shape((32, total), BF), hidden_rows, hidden_rows,
        ],
        [vmem((8, total), F32), vmem((32, total), F32)],
    )
    pools = from_peers(columns)
    partner = from_partner(lines)
    late = call(
        late_terms_kernel,
        late[:3] + [late_grad] + late[3:],
        [shape((hidden, hidden + 16)), shape((both, 32)), shape((both, 16))],
    )

    late, base = lax.optimization_barrier((late, base))
    g_early, *levels_out = call(
        functools.partial(arrive_kernel, peers),
        [base, mask, x_one, partner, codes, rows] + pools,
        [field] + sends,
    )
    above, below = from_levels(levels_out)
    base, columns, lines, early_sum, grad, second_grad, first_grad = call(
        back_kernel,
        [g_early, first, second, rows] + backward_weights,
        [
            field, column_pack, line_pack, shape((8, LANES)), shape((16, total), BF), hidden_rows,
            hidden_rows,
        ],
        [vmem((32, total), F32)],
    )
    partner = from_partner(lines)
    half = shape((hidden // 2, hidden))
    late_mid, late_wing, late_out = late
    keep, give, middle_bias = call(
        middle_kernel, [first, second_grad, late_mid], [half, half, shape((hidden, 16))]
    )
    outer = call(
        outer_kernel,
        [
            second, features, grad, first_grad, late_wing, late_out, late_sum, early_sum,
            middle_bias,
        ],
        [shape((24, hidden))],
    )[0]
    terms = keep + lax.ppermute(give, "sub", xor_pairs("sub", 1))
    terms, above, below, partner = lax.optimization_barrier((terms, above, below, partner))
    parts = from_peers(jnp.concatenate([terms, outer, columns.reshape(slots * 4, LANES)], axis=0))
    rows_sent = terms.shape[0] + outer.shape[0]
    terms = tree_sum([part[:rows_sent] for part in parts])
    mine, other = total_halves(terms)
    final_state, initial_cot, token = call(
        functools.partial(finish_kernel, rows_sent),
        [base, mask, x_two, above, below, partner, codes, rows] + parts,
        [shape(state_init.shape)] * 2 + [shape((8, LANES))],
    )
    count = (
        levels
        * lax.axis_size("depth")
        * slots
        * lax.axis_size("tiles")
        * cells
        * lax.axis_size("sub")
    )
    w_in, b_in, w_mid, b_mid, w_out, b_out = call(
        functools.partial(grads_kernel, 1.0 / math.sqrt(count)),
        [mine, other, token],
        [
            shape(weight_in.T.shape),
            shape((1, hidden)),
            shape((hidden, hidden)),
            shape((1, hidden)),
            shape(weight_out.shape),
            shape(bias_out.shape),
        ],
        scalars=1,
    )
    return (
        final_state,
        initial_cot,
        w_in.T,
        b_in.reshape(hidden),
        w_mid,
        b_mid.reshape(hidden),
        w_out,
        b_out,
    )


def solution(mesh):
    return jax.shard_map(
        body,
        mesh=mesh,
        in_specs=(
            P("groups", "depth", "tiles", "sub"),
            P("groups", "depth", "tiles", "sub"),
            P("tiles", "sub"),
            P("tiles", None),
            P("tiles", None),
            P(),
            P(),
            P(),
            P(),
            P(),
            P(),
            P(),
            P("depth"),
        ),
        out_specs=(
            P("groups", "depth", "tiles", "sub"),
            P("groups", "depth", "tiles", "sub"),
            P("groups", None),
            P("groups"),
            P("groups", None),
            P("groups"),
            P("groups", None),
            P("groups"),
        ),
        check_vma=False,
    )
```

```python
import functools
import math

import jax
import jax.numpy as jnp
from jax import lax
from jax.experimental import pallas as pl
from jax.experimental.pallas import tpu as pltpu
from jax.sharding import PartitionSpec as P

TCOL = 64
LANES = 128
CHUNK = 2048
BF = jnp.bfloat16
F32 = jnp.float32
VMEM_BYTES = 16 * 1024 * 1024
NT = (((1,), (1,)), ((), ()))


def dot(left, right):
    return jnp.dot(left, right, preferred_element_type=F32)


def dot_nt(left, right):
    return lax.dot_general(left, right, NT, preferred_element_type=F32)


def iota(shape, axis):
    return lax.broadcasted_iota(jnp.int32, shape, axis)


def wide(block, copies):
    return jnp.concatenate([block] * copies, axis=1)


def pack_columns(first, last, place_of_slot):
    place = iota((8, LANES), 1) & 63
    packed = jnp.zeros((8, LANES), F32)
    for v in range(first.shape[1] // LANES):
        span = slice(v * LANES, (v + 1) * LANES)
        at = v + place_of_slot
        low = pltpu.roll(first[:, span], at, 1) if at else first[:, span]
        high = pltpu.roll(last[:, span], at + 17, 1)
        packed = jnp.where(place == at, low, packed)
        packed = jnp.where(place == at + 16, high, packed)
    return packed


def pack_lines(first, last):
    cells = first.shape[1]
    lane = iota((8, LANES), 1)
    return jnp.where(lane < TCOL, first[:, :LANES], last[:, cells - LANES :])


def halo_fields(codes, pools, partner, slots, cells, skip=None):
    lane = iota((8, LANES), 1)
    count = cells // LANES
    east, west, lines = [], [], []

    def chosen(code, blocks):
        found = jnp.zeros((8, LANES), F32)
        for k, block in enumerate(blocks):
            found = jnp.where(code == k, block, found)
        return found

    column_blocks = []
    for pool in pools:
        for i in range(slots // 2):
            both = pool[i] if skip is None else pool[skip + 8 * i : skip + 8 * i + 8]
            column_blocks += [both, pltpu.roll(both, LANES - 32, 1)]
    line_blocks = [partner[s] for s in range(slots)]
    for s in range(slots):
        west_pack = chosen(codes[0, s], column_blocks)
        east_pack = chosen(codes[1, s], column_blocks)
        south = pltpu.roll(chosen(codes[2, s], line_blocks), TCOL, 1)
        north = pltpu.roll(chosen(codes[3, s], line_blocks), TCOL, 1)
        east += [pltpu.roll(east_pack, 63 - v, 1) for v in range(count)]
        west += [pltpu.roll(west_pack, 48 - v, 1) for v in range(count)]
        lines += [jnp.where(lane < TCOL, south, north)] * count
    return tuple(jnp.concatenate(part, axis=1) for part in (east, west, lines))


def places(shape, cells):
    lane = iota(shape, 1) & (cells - 1)
    column = lane & (TCOL - 1)
    return column == TCOL - 1, column == 0, lane >= cells - TCOL, lane < TCOL


def neighbours(x, halos, cells):
    total = x.shape[1]
    east_halo, west_halo, lines = halos
    at_east, at_west, at_north, at_south = places(x.shape, cells)
    east = jnp.where(at_east, east_halo, pltpu.roll(x, total - 1, 1))
    west = jnp.where(at_west, west_halo, pltpu.roll(x, 1, 1))
    north = jnp.where(at_north, lines, pltpu.roll(x, total - TCOL, 1))
    south = jnp.where(at_south, lines, pltpu.roll(x, TCOL, 1))
    return east, west, north, south


def halo_sum(halos, cells):
    east_halo, west_halo, lines = halos
    at_east, at_west, at_north, at_south = places(lines.shape, cells)
    columns = jnp.where(at_east, east_halo, jnp.where(at_west, west_halo, 0.0))
    return columns + jnp.where(at_north | at_south, lines, 0.0)


def pull_back(e_east, e_west, e_north, e_south, cells):
    total = e_east.shape[1]
    at_east, at_west, at_north, at_south = places(e_east.shape, cells)
    return (
        jnp.where(at_west, 0.0, pltpu.roll(e_east, 1, 1))
        + jnp.where(at_east, 0.0, pltpu.roll(e_west, total - 1, 1))
    ) + (
        jnp.where(at_south, 0.0, pltpu.roll(e_north, TCOL, 1))
        + jnp.where(at_north, 0.0, pltpu.roll(e_south, total - TCOL, 1))
    )


def write_edges(columns, lines, first_column, last_column, first_line, last_line):
    slots = lines.shape[0]
    cells = first_column.shape[1] // slots
    spans = [slice(s * cells, (s + 1) * cells) for s in range(slots)]
    packs = [
        pack_columns(first_column[:, span], last_column[:, span], 32 * (s % 2))
        for s, span in enumerate(spans)
    ]
    for s, span in enumerate(spans):
        if s % 2 == 0:
            columns[s // 2] = packs[s] + packs[s + 1]
        lines[s] = pack_lines(first_line[:, span], last_line[:, span])


def write_sends(sends, kind, x, cells):
    depth = lax.axis_index("depth")
    top = iota((8, cells), 0) < 4
    for i in range(x.shape[1] // (2 * cells)):
        even = x[:, 2 * i * cells : (2 * i + 1) * cells]
        odd = x[:, (2 * i + 1) * cells : (2 * i + 2) * cells]
        down = jnp.where(top, pltpu.roll(even, 4, 0), odd)
        up = jnp.where(top, even, pltpu.roll(odd, 4, 0))
        if len(sends) == 1:
            sends[0][kind, i] = jnp.where(depth == 0, down, up)
        else:
            sends[0][kind, i] = down
            sends[1][kind, i] = up


def level_halo(above_ref, below_ref, kind):
    depth = lax.axis_index("depth")
    last = lax.axis_size("depth") - 1
    parts = []
    for i in range(above_ref.shape[1]):
        above = jnp.where(depth > 0, above_ref[kind, i], 0.0)
        below = jnp.where(depth < last, below_ref[kind, i], 0.0)
        top = iota(above.shape, 0) < 4
        parts.append(jnp.where(top, above, pltpu.roll(below, 4, 0)))
        parts.append(jnp.where(top, pltpu.roll(above, 4, 0), below))
    return jnp.concatenate(parts, axis=1)


def start_fetch(pairs, sems):
    copies = [
        pltpu.make_async_copy(source, target, sems.at[i])
        for i, (source, target) in enumerate(pairs)
    ]
    for copy in copies:
        copy.start()
    return copies


def fetch(pairs, sems):
    for copy in start_fetch(pairs, sems):
        copy.wait()


def prep_kernel(sent, mix_v_in, state_in, cot_in, count_in, *rest):
    x_out, g_out, mask_out, columns, lines = rest[:5]
    sends = rest[5 : 5 + sent]
    mix_v, state, cot, count, sems = rest[5 + sent :]
    copies = start_fetch(
        [(mix_v_in, mix_v), (count_in, count), (state_in, state), (cot_in, cot)], sems
    )
    for copy in copies[:3]:
        copy.wait()
    slots = state.shape[2]
    cells = state.shape[3]
    depth = lax.axis_index("depth")
    for s in range(slots):
        span = slice(s * cells, (s + 1) * cells)
        for l in range(2):
            for f in range(4):
                r = 4 * l + f
                x_out[r : r + 1, span] = state[f, l, s : s + 1, :]
    deep = jnp.concatenate(
        [jnp.broadcast_to(count[s : s + 1, :], (8, cells)) for s in range(slots)], axis=1
    )
    upper = iota(deep.shape, 0) < 4
    mask = jnp.where(2 * depth + jnp.where(upper, 0, 1) < deep, 1.0, 0.0)
    x = mask * x_out[...]
    mask_out[...] = mask
    x_out[...] = x
    write_edges(columns, lines, x, x, x, x)
    write_sends(sends, 0, x, cells)
    copies[3].wait()
    for s in range(slots):
        span = slice(s * cells, (s + 1) * cells)
        for l in range(2):
            for f in range(4):
                r = 4 * l + f
                g_out[r : r + 1, span] = cot[f, l, s : s + 1, :]
    g = mask * g_out[...]
    g_out[...] = g
    write_sends(sends, 1, jnp.where(upper, mix_v[0], mix_v[1]) * g, cells)


def weight_kernel(
    mix_h_in, mix_v_in, bias_out_in, we_in, sn_in, w_in_in, b_in_in, w_mid_in, b_mid_in, w_out_in,
    in_all, in_back, mid_all, mid_back, bias_mid, out_all, out_back, rows, codes,
    mix_h, mix_v, bias_out, we, sn, w_in, b_in, w_mid, b_mid, w_out, sems
):
    fetch(
        [
            (mix_h_in, mix_h), (mix_v_in, mix_v), (bias_out_in, bias_out), (we_in, we),
            (sn_in, sn), (w_in_in, w_in), (b_in_in, b_in), (w_mid_in, w_mid), (b_mid_in, b_mid),
            (w_out_in, w_out),
        ],
        sems,
    )
    hidden = w_mid.shape[0]
    feature = w_in.shape[0]
    high = b_in[...].astype(BF).astype(F32)
    low = b_in[...] - high
    row = iota((32, hidden), 0)
    halves = []
    for l in range(2):
        r = iota((32, feature), 0)
        c = iota((32, feature), 1)
        chosen = (r < 24) & (((r >> 2) & 1) == l) & ((r >> 3) * 4 + (r & 3) == c)
        part = dot(jnp.where(chosen, 1.0, 0.0).astype(BF), w_in[...])
        part = jnp.where(row == 24, high, jnp.where(row == 25, low, part))
        halves.append(part)
    both = jnp.concatenate(halves, axis=1)
    in_back[...] = both.astype(BF)
    padded = jnp.concatenate([both, jnp.zeros((96, 2 * hidden), F32)], axis=0)
    in_all[...] = padded.T[:, :32].astype(BF)
    middle = w_mid[...].astype(F32)
    turned = middle.T
    zero = jnp.zeros((hidden, hidden), F32)
    for source, target in ((middle, mid_all), (turned, mid_back)):
        target[...] = jnp.concatenate(
            [jnp.concatenate([source, zero], axis=1), jnp.concatenate([zero, source], axis=1)],
            axis=0,
        ).astype(BF)
    column = jnp.broadcast_to(b_mid[...], (hidden, hidden)).T
    bias_mid[...] = jnp.concatenate([column, column], axis=0)
    out = w_out[...].astype(F32)
    empty = jnp.zeros((4, hidden), F32)
    upper = jnp.concatenate([out, empty], axis=0)
    lower = jnp.concatenate([empty, out], axis=0)
    wide_out = jnp.concatenate(
        [jnp.concatenate([upper, lower], axis=1), jnp.zeros((120, 2 * hidden), F32)], axis=0
    )
    out_all[...] = wide_out[:16].astype(BF)
    out_back[...] = wide_out.T[:, :16].astype(BF)
    r8 = iota((8, LANES), 0)
    f8 = r8 & 3

    def by_field(scalars):
        return jnp.where(
            f8 == 0,
            scalars[0],
            jnp.where(f8 == 1, scalars[1], jnp.where(f8 == 2, scalars[2], scalars[3])),
        )

    rows[0] = by_field(mix_h)
    rows[1] = jnp.where(r8 < 4, mix_v[0], mix_v[1])
    rows[2] = by_field(bias_out)
    here = lax.axis_index("tiles")
    half = lax.axis_index("sub")
    slots = codes.shape[1]
    for s in range(slots):
        for side in range(2):
            tile = we[side, s]
            safe = jnp.maximum(tile, 0)
            owner = jnp.bitwise_xor(lax.div(safe, slots), here)
            code = jnp.where(tile >= 0, owner * slots + lax.rem(safe, slots), -1)
            codes[side, s] = jnp.full((8, LANES), code, jnp.int32)
            code = jnp.where(half == side, sn[side, s], s)
            codes[2 + side, s] = jnp.full((8, LANES), code, jnp.int32)


def stencil(x, halos, cells):
    east, west, north, south = neighbours(x, halos, cells)
    diffuse = (east + west) + (north + south) - 4.0 * x
    ones = jnp.where(iota(x.shape, 0) < 2, 1.0, 0.0)
    features = jnp.concatenate([x, east - west, north - south, ones], axis=0).astype(BF)
    return diffuse, features


def keep_first(first_out, span, first):
    hidden = first.shape[0] // 2
    ones = jnp.ones((16, first.shape[1]), BF)
    for l in range(2):
        base = l * (hidden + 16)
        first_out[base : base + hidden, span] = first[l * hidden : (l + 1) * hidden]
        first_out[base + hidden : base + hidden + 16, span] = ones


def forward_kernel(
    peers, x_in, mask, above, below, partner, codes, in_all, mid_all, bias_mid, out_all, rows,
    *rest
):
    pools = rest[:peers]
    x_out, first_out, second_out, feature_out, columns, lines, closure = rest[peers:]
    slots = partner.shape[0]
    x = x_in[...]
    total = x.shape[1]
    cells = total // slots
    halos = halo_fields(codes, pools, partner, slots, cells)
    diffuse, features = stencil(x, halos, cells)
    feature_out[...] = features
    bias = wide(bias_mid[...], CHUNK // LANES)
    for start in range(0, total, CHUNK):
        span = slice(start, start + CHUNK)
        first = jnp.tanh(dot(in_all[...], feature_out[:, span])).astype(BF)
        keep_first(first_out, span, first)
        second = jnp.tanh(dot(mid_all[...], first) + bias).astype(BF)
        second_out[:, span] = second
        closure[:, span] = dot(out_all[...], second)[:8]
    mh, mv, bo = (wide(rows[k], total // LANES) for k in range(3))
    vertical = pltpu.roll(x, 4, 0) + level_halo(above, below, 0)
    x_new = mask[...] * (x + mh * diffuse + mv * (vertical - 2.0 * x) + (closure[...] + bo))
    x_out[...] = x_new
    write_edges(columns, lines, x_new, x_new, x_new, x_new)


def backward_tail(g, grad_feature, remote, rows, base, columns, lines, g_sum):
    total = g.shape[1]
    many = total // LANES
    cells = total // lines.shape[0]
    mh = wide(rows[0], many)
    mv = wide(rows[1], many)
    along = mh * g
    e_east = along + grad_feature[8:16]
    e_west = along - grad_feature[8:16]
    e_north = along + grad_feature[16:24]
    e_south = along - grad_feature[16:24]
    spread = mv * g
    vertical = pltpu.roll(spread, 4, 0) - 2.0 * spread
    if remote is not None:
        vertical = vertical + remote
    write_edges(columns, lines, e_west, e_east, e_south, e_north)
    base[...] = (
        (g + grad_feature[0:8])
        + (pull_back(e_east, e_west, e_north, e_south, cells) - 4.0 * along)
        + vertical
    )
    sums = [g[:, v * LANES : (v + 1) * LANES] for v in range(many)]
    g_sum[...] = tree_sum(sums)


def grad_rows(g):
    return jnp.concatenate([g, jnp.zeros(g.shape, F32)], axis=0).astype(BF)


def seed_kernel(g_in, out_back, grad_out, seed_out):
    grad_out[...] = grad_rows(g_in[...])
    total = g_in.shape[1]
    for start in range(0, total, CHUNK):
        span = slice(start, start + CHUNK)
        seed_out[:, span] = dot(out_back[...], grad_out[:, span]).astype(BF)


def turn_kernel(
    peers, x_in, mask, g_in, seed, above, below, partner, codes, in_all, mid_all, bias_mid,
    out_all, rows, mid_back, in_back, *rest
):
    pools = rest[:peers]
    (
        x_out, base, columns, lines, g_sum, first_out, second_out, feature_out,
        second_grad_out, first_grad_out, closure, grad_feature,
    ) = rest[peers:]
    slots = partner.shape[0]
    x = x_in[...]
    g = g_in[...]
    total = x.shape[1]
    cells = total // slots
    halos = halo_fields(codes, pools, partner, slots, cells)
    diffuse, features = stencil(x, halos, cells)
    feature_out[...] = features
    bias = wide(bias_mid[...], CHUNK // LANES)
    for start in range(0, total, CHUNK):
        span = slice(start, start + CHUNK)
        first = jnp.tanh(dot(in_all[...], feature_out[:, span])).astype(BF)
        keep_first(first_out, span, first)
        second = jnp.tanh(dot(mid_all[...], first) + bias).astype(BF)
        second_out[:, span] = second
        closure[:, span] = dot(out_all[...], second)[:8]
        second_grad = times_slope(seed[:, span], second)
        second_grad_out[:, span] = second_grad
        first_grad = times_slope(dot(mid_back[...], second_grad), first)
        first_grad_out[:, span] = first_grad
        grad_feature[:, span] = dot(in_back[...], first_grad)
    remote = level_halo(above, below, 1)
    backward_tail(g, grad_feature[...], remote, rows, base, columns, lines, g_sum)
    mh, mv, bo = (wide(rows[k], total // LANES) for k in range(3))
    x_out[...] = mask[...] * (
        x + mh * diffuse + mv * (pltpu.roll(x, 4, 0) - 2.0 * x) + (closure[...] + bo)
    )


def times_slope(grad, value):
    return grad.astype(BF) * (1.0 - value * value)


def arrive_kernel(peers, base_in, mask, x_in, partner, codes, rows, *rest):
    pools = rest[:peers]
    g_out = rest[peers]
    sends = rest[peers + 1 :]
    slots = partner.shape[0]
    total = base_in.shape[1]
    cells = total // slots
    halos = halo_fields(codes, pools, partner, slots, cells)
    g = mask[...] * (base_in[...] + halo_sum(halos, cells))
    g_out[...] = g
    write_sends(sends, 0, x_in[...], cells)
    write_sends(sends, 1, wide(rows[1], total // LANES) * g, cells)


def back_kernel(
    g_in, first_in, second_in, rows, out_back, mid_back, in_back, base, columns, lines, g_sum,
    grad_out, second_grad_out, first_grad_out, grad_feature
):
    g = g_in[...]
    total = g.shape[1]
    hidden = mid_back.shape[0] // 2
    grad_out[...] = grad_rows(g)
    for start in range(0, total, CHUNK):
        span = slice(start, start + CHUNK)
        first = jnp.concatenate(
            [first_in[:hidden, span], first_in[hidden + 16 : 2 * hidden + 16, span]], axis=0
        )
        second_grad = times_slope(dot(out_back[...], grad_out[:, span]), second_in[:, span])
        second_grad_out[:, span] = second_grad
        first_grad = times_slope(dot(mid_back[...], second_grad), first)
        first_grad_out[:, span] = first_grad
        grad_feature[:, span] = dot(in_back[...], first_grad)
    backward_tail(g, grad_feature[...], None, rows, base, columns, lines, g_sum)


def middle_sums(first, second_grad):
    hidden = first.shape[0] // 2 - 16
    side = hidden + 16
    return dot_nt(second_grad[:hidden], first[:side]) + dot_nt(second_grad[hidden:], first[side:])


def outer_sums(second, features, grad, first_grad):
    return dot_nt(first_grad[...], features[...]), dot_nt(second[...], grad[...])


def late_terms_kernel(first, second, features, grad, second_grad, first_grad, mid, wing, out):
    mid[...] = middle_sums(first, second_grad)
    wing[...], out[...] = outer_sums(second, features, grad, first_grad)


def middle_kernel(first, second_grad, late, keep, send, bias):
    total = late[...] + middle_sums(first, second_grad)
    half, hidden = keep.shape
    core = lax.axis_index("sub")
    low, high = total[:half, :hidden], total[half:, :hidden]
    keep[...] = jnp.where(core == 0, low, high)
    send[...] = jnp.where(core == 0, high, low)
    bias[...] = total[:, hidden:]


def outer_kernel(
    second, features, grad, first_grad, late_wing, late_out, late_sum, early_sum, middle_bias,
    packed
):
    wing, out = outer_sums(second, features, grad, first_grad)
    wing = wing + late_wing[...]
    out = out + late_out[...]
    total = late_sum[...] + early_sum[...]
    hidden = wing.shape[0] // 2
    top = iota((8, hidden), 0)

    def turned(block):
        blank = jnp.zeros((block.shape[0], hidden - block.shape[1]), F32)
        return jnp.concatenate([block, blank], axis=1).T

    low, high = turned(wing[:hidden]), turned(wing[hidden:])
    kinds = [low[8 * k : 8 * k + 8] + pltpu.roll(high[8 * k : 8 * k + 8], 4, 0) for k in range(3)]
    bias_in = low[24:32] + high[24:32]
    bias_mid = turned(middle_bias[...])[:8]
    biases = jnp.where(top == 4, pltpu.roll(bias_in, 4, 0), pltpu.roll(bias_mid, 5, 0))
    low, high = turned(out[:hidden]), turned(out[hidden:])
    packed[0:8] = jnp.where(top < 4, kinds[0], pltpu.roll(kinds[1], 4, 0))
    packed[8:16] = jnp.where(top < 4, kinds[2], biases)
    packed[16:24] = jnp.where(
        top < 4, low[:8] + pltpu.roll(high[:8], 4, 0), total + pltpu.roll(total, 4, 0)
    )


def finish_kernel(skip, base_in, mask, x_in, above, below, partner, codes, rows, *rest):
    pools = rest[:-3]
    final, initial, token = rest[-3:]
    token[...] = jnp.zeros(token.shape, F32)
    slots = partner.shape[0]
    total = base_in.shape[1]
    cells = total // slots
    mv = wide(rows[1], total // LANES)
    halos = halo_fields(codes, pools, partner, slots, cells, skip)
    last = x_in[...] + mask[...] * (mv * level_halo(above, below, 0))
    early = mask[...] * ((base_in[...] + level_halo(above, below, 1)) + halo_sum(halos, cells))
    for s in range(slots):
        span = slice(s * cells, (s + 1) * cells)
        for l in range(2):
            for f in range(4):
                r = 4 * l + f
                final[f, l, s : s + 1, :] = last[r : r + 1, span]
                initial[f, l, s : s + 1, :] = early[r : r + 1, span]


def grads_kernel(scale, mine, other, token, w_in, b_in, w_mid, b_mid, w_out, b_out):
    hidden = w_mid.shape[0]
    core = lax.axis_index("sub")
    half = hidden // 2
    w_mid[:half] = jnp.where(core == 0, mine[:half], other[:half]) * scale
    w_mid[half:] = jnp.where(core == 0, other[:half], mine[:half]) * scale
    tail = (mine[half:] + other[half:]) * scale
    w_in[...] = tail[0:12]
    b_in[...] = tail[12:13]
    b_mid[...] = tail[13:14]
    w_out[...] = tail[16:20]
    for f in range(4):
        b_out[f] = jnp.sum(tail[20 + f : 21 + f])


def call(kernel, inputs, outs, scratch=(), spaces=None, scalars=0):
    if spaces is not None:
        inputs = [pltpu.with_memory_space_constraint(array, spaces) for array in inputs]
    return pl.pallas_call(
        kernel,
        in_specs=[pl.BlockSpec(memory_space=spaces or pltpu.VMEM)] * len(inputs),
        out_specs=[pl.BlockSpec(memory_space=pltpu.VMEM)] * (len(outs) - scalars)
        + [pl.BlockSpec(memory_space=pltpu.SMEM)] * scalars,
        out_shape=outs,
        scratch_shapes=list(scratch),
        compiler_params=pltpu.CompilerParams(vmem_limit_bytes=VMEM_BYTES),
    )(*inputs)


def shape(dims, dtype=F32):
    return jax.ShapeDtypeStruct(tuple(dims), dtype)


def xor_pairs(axis, k):
    return [(i, i ^ k) for i in range(lax.axis_size(axis))]


def from_peers(packs):
    return [packs] + [
        lax.ppermute(packs, "tiles", xor_pairs("tiles", k))
        for k in range(1, lax.axis_size("tiles"))
    ]


def from_partner(lines):
    return lax.ppermute(lines, "sub", xor_pairs("sub", 1))


def from_levels(sends):
    depth = lax.axis_size("depth")
    if len(sends) == 1:
        other = lax.ppermute(sends[0], "depth", [(0, 1), (1, 0)])
        return other, other
    down = [(i, i + 1) for i in range(depth - 1)]
    return (
        lax.ppermute(sends[0], "depth", down),
        lax.ppermute(sends[1], "depth", [(j, i) for i, j in down]),
    )


def tree_sum(parts):
    while len(parts) > 1:
        parts = [parts[i] + parts[i + 1] for i in range(0, len(parts), 2)]
    return parts[0]


def sum_over(array, axis):
    return tree_sum(
        [array]
        + [lax.ppermute(array, axis, xor_pairs(axis, k)) for k in range(1, lax.axis_size(axis))]
    )


def total_halves(terms):
    if lax.axis_size("depth") > 2:
        mine = sum_over(terms, "depth")
        return mine, lax.ppermute(mine, "sub", xor_pairs("sub", 1))
    crossed = lax.ppermute(terms, ("depth", "sub"), [(i, i ^ 3) for i in range(4)])
    below = lax.ppermute(terms, "depth", xor_pairs("depth", 1))
    beside = lax.ppermute(terms, "sub", xor_pairs("sub", 1))
    return terms + below, beside + crossed


def body(
    state_init,
    cotangent,
    level_count,
    west_east,
    south_north,
    weight_in,
    bias_in,
    weight_mid,
    bias_mid,
    weight_out,
    bias_out,
    mix_horizontal,
    mix_vertical,
):
    _, levels, slots, cells = state_init.shape
    hidden = weight_mid.shape[0]
    both = 2 * hidden
    total = slots * cells
    peers = lax.axis_size("tiles")
    field = shape((8, total))
    column_pack = shape((slots // 2, 8, LANES))
    line_pack = shape((slots, 8, LANES))
    sends = [shape((2, slots // 2, 8, cells))] * (1 if lax.axis_size("depth") == 2 else 2)
    hidden_rows = shape((both, total), BF)
    first_rows = shape((both + 32, total), BF)
    vmem, smem = pltpu.VMEM, pltpu.SMEM

    inputs = [mix_vertical, state_init, cotangent, level_count]
    x_zero, g_late, mask, columns, lines, *levels_out = call(
        functools.partial(prep_kernel, len(sends)),
        inputs,
        [field, field, field, column_pack, line_pack] + sends,
        [
            smem(mix_vertical.shape, F32),
            vmem(state_init.shape, F32),
            vmem(cotangent.shape, F32),
            vmem(level_count.shape, jnp.int32),
            pltpu.SemaphoreType.DMA((len(inputs),)),
        ],
        pltpu.HBM,
    )
    above, below = from_levels(levels_out)
    pools = from_peers(columns)
    partner = from_partner(lines)

    inputs = [
        mix_horizontal,
        mix_vertical,
        bias_out,
        west_east.T,
        south_north.T,
        weight_in.T,
        bias_in.reshape(1, hidden),
        weight_mid,
        bias_mid.reshape(1, hidden),
        weight_out,
    ]
    in_all, in_back, mid_all, mid_back, mid_bias, out_all, out_back, rows, codes = call(
        weight_kernel,
        inputs,
        [
            shape((both, 32), BF),
            shape((32, both), BF),
            shape((both, both), BF),
            shape((both, both), BF),
            shape((both, hidden)),
            shape((16, both), BF),
            shape((both, 16), BF),
            shape((3, 8, LANES)),
            shape((4, slots, 8, LANES), jnp.int32),
        ],
        [(smem if i < 5 else vmem)(a.shape, a.dtype) for i, a in enumerate(inputs)]
        + [pltpu.SemaphoreType.DMA((len(inputs),))],
        pltpu.HBM,
    )
    forward_weights = [in_all, mid_all, mid_bias, out_all, rows]
    backward_weights = [out_back, mid_back, in_back]

    late_grad, seed = call(seed_kernel, [g_late, out_back], [shape((16, total), BF), hidden_rows])

    x_one, first, second, features, columns, lines = call(
        functools.partial(forward_kernel, peers),
        [x_zero, mask, above, below, partner, codes] + forward_weights + pools,
        [field, first_rows, hidden_rows, shape((32, total), BF), column_pack, line_pack],
        [vmem((8, total), F32)],
    )
    pools = from_peers(columns)
    partner = from_partner(lines)

    x_two, base, columns, lines, late_sum, *late = call(
        functools.partial(turn_kernel, peers),
        [x_one, mask, g_late, seed, above, below, partner, codes]
        + forward_weights
        + backward_weights[1:]
        + pools,
        [
            field, field, column_pack, line_pack, shape((8, LANES)), first_rows, hidden_rows,
            shape((32, total), BF), hidden_rows, hidden_rows,
        ],
        [vmem((8, total), F32), vmem((32, total), F32)],
    )
    pools = from_peers(columns)
    partner = from_partner(lines)
    late = call(
        late_terms_kernel,
        late[:3] + [late_grad] + late[3:],
        [shape((hidden, hidden + 16)), shape((both, 32)), shape((both, 16))],
    )

    late, base = lax.optimization_barrier((late, base))
    g_early, *levels_out = call(
        functools.partial(arrive_kernel, peers),
        [base, mask, x_one, partner, codes, rows] + pools,
        [field] + sends,
    )
    above, below = from_levels(levels_out)
    base, columns, lines, early_sum, grad, second_grad, first_grad = call(
        back_kernel,
        [g_early, first, second, rows] + backward_weights,
        [
            field, column_pack, line_pack, shape((8, LANES)), shape((16, total), BF), hidden_rows,
            hidden_rows,
        ],
        [vmem((32, total), F32)],
    )
    partner = from_partner(lines)
    half = shape((hidden // 2, hidden))
    late_mid, late_wing, late_out = late
    keep, give, middle_bias = call(
        middle_kernel, [first, second_grad, late_mid], [half, half, shape((hidden, 16))]
    )
    outer = call(
        outer_kernel,
        [
            second, features, grad, first_grad, late_wing, late_out, late_sum, early_sum,
            middle_bias,
        ],
        [shape((24, hidden))],
    )[0]
    terms = keep + lax.ppermute(give, "sub", xor_pairs("sub", 1))
    terms, above, below, partner = lax.optimization_barrier((terms, above, below, partner))
    parts = from_peers(jnp.concatenate([terms, outer, columns.reshape(slots * 4, LANES)], axis=0))
    rows_sent = terms.shape[0] + outer.shape[0]
    terms = tree_sum([part[:rows_sent] for part in parts])
    mine, other = total_halves(terms)
    final_state, initial_cot, token = call(
        functools.partial(finish_kernel, rows_sent),
        [base, mask, x_two, above, below, partner, codes, rows] + parts,
        [shape(state_init.shape)] * 2 + [shape((8, LANES))],
    )
    count = (
        levels
        * lax.axis_size("depth")
        * slots
        * lax.axis_size("tiles")
        * cells
        * lax.axis_size("sub")
    )
    w_in, b_in, w_mid, b_mid, w_out, b_out = call(
        functools.partial(grads_kernel, 1.0 / math.sqrt(count)),
        [mine, other, token],
        [
            shape(weight_in.T.shape),
            shape((1, hidden)),
            shape((hidden, hidden)),
            shape((1, hidden)),
            shape(weight_out.shape),
            shape(bias_out.shape),
        ],
        scalars=1,
    )
    return (
        final_state,
        initial_cot,
        w_in.T,
        b_in.reshape(hidden),
        w_mid,
        b_mid.reshape(hidden),
        w_out,
        b_out,
    )


def solution(mesh):
    return jax.shard_map(
        body,
        mesh=mesh,
        in_specs=(
            P("groups", "depth", "tiles", "sub"),
            P("groups", "depth", "tiles", "sub"),
            P("tiles", "sub"),
            P("tiles", None),
            P("tiles", None),
            P(),
            P(),
            P(),
            P(),
            P(),
            P(),
            P(),
            P("depth"),
        ),
        out_specs=(
            P("groups", "depth", "tiles", "sub"),
            P("groups", "depth", "tiles", "sub"),
            P("groups", None),
            P("groups"),
            P("groups", None),
            P("groups"),
            P("groups", None),
            P("groups"),
        ),
        check_vma=False,
    )
```
